512 devices in a mesh: seq: 16 (over y_lo, x, core), ctx: 32 (over y_hi, z).
Axes of the slice: x: 4, y: 4 (y_hi: 2, y_lo: 2; y = y_hi * 2 + y_lo), z: 16, core: 2. Of those that a mesh axis runs over, the one named last changes fastest.
Arguments:
- queries: bfloat16 [65536, 1536], P(('ctx', 'seq')), may hold values from -6 to 6
- key_rows: bfloat16 [65536, 1536], P(('ctx', 'seq')), may hold values from -6 to 6
- value_rows: bfloat16 [65536, 1536], P(('ctx', 'seq')), may hold values from -24 to 24
- block_in: bfloat16 [65536, 1536], P(('ctx', 'seq')), may hold values from -6 to 6
- grad_out: bfloat16 [65536, 1536], P(('ctx', 'seq')), may hold values from -12 to 12
- conv_kernel: float32 [32, 1536], replicated, may hold values from -1 to 1
- drop_bits: int32 [2048, 16], P(('ctx', 'seq')), may hold values from -2147483648 to 2147483647, as said below
- seg_length: int32 [32], P('ctx'), may hold values from 1024 to 2048, as said below
Outputs:
- grad_queries: bfloat16 [65536, 1536], P(('ctx', 'seq'))
- grad_keys: bfloat16 [65536, 1536], P(('ctx', 'seq'))
- grad_values: bfloat16 [65536, 1536], P(('ctx', 'seq'))
- grad_block: bfloat16 [65536, 1536], P(('ctx', 'seq'))
- grad_kernel: float32 [32, 1536], replicated
The draws below stay inside these ranges and needn't reach their ends.
Inputs may be any that keep to these rules, and one draw needn't show every extreme that they name: `drop_bits`: each word holds one head's bits of 32 consecutive frames, frame 32 * i + b of row i in bit b; a set bit drops the frame's head output. `seg_length`: some segment is full and some holds exactly 1024 live frames; live frames come first in a segment.
All inputs are finite; a program needn't handle non-finite values.
Results may differ from the reference program's by a relative error of at most 0.0081.
Values may be sent and summed in bfloat16 or wider, within the bound.
A program may use at most 64 MiB of HBM per device.

```python
import math
import jax
import jax.numpy as jnp
from jax import lax

HD = 96
KW = 32
HEADS = 16
D = 1536
SEG = 2048
SEGS = 32
FRAMES = 65536


def draw_queries(key, part):
    own_key = jax.random.fold_in(key, 11)
    base = jnp.clip(1.25 * jax.random.normal(own_key, (SEGS, SEG, D), jnp.float32), -6.0, 6.0)
    return base.reshape(FRAMES, D).astype(jnp.bfloat16)


def draw_key_rows(key, part):
    own_key = jax.random.fold_in(key, 17)
    base = jnp.clip(1.25 * jax.random.normal(own_key, (SEGS, SEG, D), jnp.float32), -6.0, 6.0)
    return base.reshape(FRAMES, D).astype(jnp.bfloat16)


def random_words(key):
    high_key, low_key = jax.random.split(key)
    high_part = jax.random.randint(high_key, (FRAMES // 32, HEADS), -32768, 32768)
    low_part = jax.random.randint(low_key, (FRAMES // 32, HEADS), 0, 65536)
    return high_part * 65536 + low_part


def draw_drop_bits(key, part):
    key = jax.random.fold_in(key, 31)
    first_key, second_key = jax.random.split(key)
    return jnp.bitwise_and(random_words(first_key), random_words(second_key)).astype(jnp.int32)


def draw_seg_length(key, part):
    key = jax.random.fold_in(key, 41)
    length_key, order_key = jax.random.split(key)
    lengths = jax.random.randint(length_key, (SEGS,), SEG // 2, SEG + 1)
    order = jax.random.permutation(order_key, SEGS)
    lengths = jnp.where(order == 0, SEG, lengths)
    lengths = jnp.where(order == 1, SEG // 2, lengths)
    return lengths.astype(jnp.int32)


def level_of(stream_key, shape, cuts, least, largest):
    level, own = 1.0, jax.random.fold_in(stream_key, 6)
    for dim, blocks in cuts:
        draws = jnp.exp(jax.random.uniform(jax.random.fold_in(own, dim), (blocks,), jnp.float32, least / len(cuts), largest / len(cuts)))
        level = level * jnp.repeat(draws, shape[dim] // blocks).reshape([-1 if axis == dim else 1 for axis in range(len(shape))])
    return level


def noise(rng, extent, width, bound, cuts=(), kind=jnp.bfloat16):
    loudness = level_of(rng, extent, cuts, -0.22, 0.18) if cuts else 1.0
    values = jax.random.normal(rng, extent, jnp.float32) * width * loudness
    return jnp.minimum(jnp.maximum(values, -bound), bound).astype(kind)


def setup_inputs(seed: int = 0) -> dict:
    keys = jax.random.split(jax.random.key(seed), 9)
    return {
        "queries": draw_queries(jax.random.fold_in(keys[8], 71), 0),
        "key_rows": draw_key_rows(jax.random.fold_in(keys[8], 71), 0),
        "value_rows": noise(keys[2], (FRAMES, D), 4.0, 24.0, ((0, 512),)),
        "block_in": noise(keys[3], (FRAMES, D), 1.0, 6.0, ((0, 512),)),
        "grad_out": noise(keys[4], (FRAMES, D), 2.0, 12.0, ((0, 512),)),
        "conv_kernel": noise(keys[5], (KW, D), KW ** -0.5, 1.0, (), jnp.float32),
        "drop_bits": draw_drop_bits(jax.random.fold_in(keys[8], 71), 0),
        "seg_length": draw_seg_length(jax.random.fold_in(keys[8], 71), 0),
    }


def unpack_bits(words):
    shifts = jnp.arange(32, dtype=jnp.int32)
    planes = jnp.right_shift(words[:, None, :], shifts[None, :, None]) & 1
    return planes.reshape(words.shape[0] * 32, words.shape[1])

def taps(padded, kernel, count):
    total = jnp.zeros((count, padded.shape[1]), jnp.float32)
    for offset in range(kernel.shape[0]):
        total = total + kernel[offset] * padded[offset:offset + count].astype(jnp.float32)
    return total

def slope_of(pre_act):
    sigma = jax.nn.sigmoid(pre_act)
    return sigma * (1.0 + pre_act * (1.0 - sigma))

def head_backward(items):
    query_rows, key_part, value_part, grad_attn, live_keys = items
    scale = 1.0 / math.sqrt(query_rows.shape[1])
    scores = jnp.dot(query_rows, key_part.T, preferred_element_type=jnp.float32) * scale
    scores = jnp.where(live_keys[None, :] > 0, scores, -1e+30)
    highest = lax.optimization_barrier(jnp.max(scores, axis=1, keepdims=True))
    raised = jnp.exp(scores - highest)
    prob = raised / lax.optimization_barrier(jnp.sum(raised, axis=1, keepdims=True))
    prob_half = prob.astype(jnp.bfloat16)
    grad_value = jnp.dot(prob_half.T, grad_attn, preferred_element_type=jnp.float32).astype(jnp.bfloat16)
    grad_prob = jnp.dot(grad_attn, value_part.T, preferred_element_type=jnp.float32)
    delta = lax.optimization_barrier(jnp.sum(prob * grad_prob, axis=1, keepdims=True))
    grad_scores = (prob * (grad_prob - delta) * scale).astype(jnp.bfloat16)
    grad_query = jnp.dot(grad_scores, key_part, preferred_element_type=jnp.float32).astype(jnp.bfloat16)
    grad_key = jnp.dot(grad_scores.T, query_rows, preferred_element_type=jnp.float32).astype(jnp.bfloat16)
    return (grad_query, grad_key, grad_value)

def to_heads(array):
    return array.reshape(SEGS, SEG, HEADS, HD).transpose(0, 2, 1, 3).reshape(SEGS * HEADS, SEG, HD)

def from_heads(array):
    return array.reshape(SEGS, HEADS, SEG, HD).transpose(0, 2, 1, 3).reshape(FRAMES, D)

def reference(queries, key_rows, value_rows, block_in, grad_out, conv_kernel, drop_bits, seg_length):
    padded = jnp.pad(block_in.astype(jnp.float32), ((15, 16), (0, 0)))
    pre_act = taps(padded, conv_kernel, FRAMES)
    grad_wide = grad_out.astype(jnp.float32)
    grad_conv = (grad_wide * slope_of(pre_act)).astype(jnp.bfloat16)
    conv_wide = grad_conv.astype(jnp.float32)
    grad_pad = jnp.pad(conv_wide, ((16, 15), (0, 0)))
    grad_in = grad_wide + taps(grad_pad, conv_kernel[::-1], FRAMES)
    grad_kernel = jnp.stack([lax.optimization_barrier(jnp.sum(padded[offset:offset + FRAMES] * conv_wide, axis=0)) for offset in range(KW)]) / SEGS
    position = jnp.arange(FRAMES, dtype=jnp.int32)
    live = (position % SEG < seg_length[position // SEG]).astype(jnp.float32)
    dropped = unpack_bits(drop_bits)
    keep = (1 - dropped).astype(jnp.float32) * (4.0 / 3.0)
    grad_attn = (grad_in.reshape(FRAMES, HEADS, HD) * keep[:, :, None] * live[:, None, None]).astype(jnp.bfloat16)
    live_keys = jnp.repeat(live.reshape(SEGS, SEG), HEADS, axis=0)
    results = lax.map(head_backward, (to_heads(queries), to_heads(key_rows), to_heads(value_rows), to_heads(grad_attn.reshape(FRAMES, D)), live_keys))
    return (from_heads(results[0]), from_heads(results[1]), from_heads(results[2]), grad_in.astype(jnp.bfloat16), grad_kernel)
```

```python
import functools
import math

import jax
import jax.numpy as jnp
from jax import lax
from jax.experimental import pallas as pl
from jax.experimental.pallas import tpu as pltpu
from jax.sharding import PartitionSpec as P

BF = jnp.bfloat16
F32 = jnp.float32
HD = 96
HEADS = 16
ROWS = 128
WIDTH = HEADS * HD
SEG = 2048
TAPS = 32
LANES = 128
GROUPS = WIDTH // LANES
QB = 256
NB = SEG // QB
NZ = 16
SCALE = 1.0 / math.sqrt(HD)
EXP2_SCALE = SCALE * math.log2(math.e)
MESH = pl.DeviceIdType.MESH


def dot(a, b):
    return lax.dot_general(a, b, (((1,), (0,)), ((), ())), preferred_element_type=F32)


def block(index, size):
    return pl.ds(pl.multiple_of(index * size, size), size)


def halves(x):
    return [x[:, c * LANES : (c + 1) * LANES] for c in range(x.shape[1] // LANES)]


def kernel(
    q_ref, k_ref, v_ref, x_ref, go_ref, taps_ref, bits_ref, len_ref,
    dq_ref, dk_ref, dv_ref, gb_ref, gk_ref,
    x_pad, g_pad, go_wide, gi_wide, rim_out, x_rim, g_rim, keep_t,
    part, pair_in, half, z_in, chip_out, chip_in, full_out, full_z, full_pair,
    q_loc, k_loc, v_loc, a_loc, q_t, k_t, v_t, a_t,
    q_n, k_n, a_n, k_aug, v_aug, prob, dscore, work, inv_ref, side,
    dq_t, dk_t, dv_t, dq_in, dk_in, dv_in,
    in_send, in_recv, out_send, out_recv, rim_send, rim_recv, sum_send, sum_recv,
):
    seq = lax.axis_index("seq")
    ctx = lax.axis_index("ctx")
    chip = seq // 2
    core = seq % 2
    sibling = chip * 2 + (1 - core)
    y_hi = ctx // NZ
    z = ctx % NZ
    here = y_hi * 8 + chip
    place = ctx * 16 + seq
    total = 512
    before = lax.rem(place + total - 1, total)
    after = lax.rem(place + 1, total)
    before_id = (before % 16, before // 16)
    after_id = (after % 16, after // 16)
    length = len_ref[0]

    def remote(src, dst, send, recv, device):
        return pltpu.make_async_remote_copy(
            src_ref=src, dst_ref=dst, send_sem=send, recv_sem=recv,
            device_id=device, device_id_type=MESH,
        )

    def to_chip(r):
        other = lax.rem(here + r, 16)
        return ((other % 8) * 2 + core, (other // 8) * NZ + z)

    barrier = pltpu.get_barrier_semaphore()

    def greet(device):
        pl.semaphore_signal(barrier, inc=1, device_id=device, device_id_type=MESH)

    greet(before_id)
    greet(after_id)

    def greet_some(r, carry):
        greet((lax.rem(seq + r, 16), ctx))
        greet((seq, y_hi * NZ + lax.rem(z + r, NZ)))
        return carry

    lax.fori_loop(1, 16, greet_some, 0)

    def greet_far(r, carry):
        greet((r * 2 + core, (1 - y_hi) * NZ + z))
        return carry

    lax.fori_loop(0, 8, greet_far, 0)

    def turn(src, dst):
        for j in range(GROUPS):
            s = slice(j * LANES, (j + 1) * LANES)
            dst[s, :] = src[:, s].T

    def send_in(n, loc, got):
        def one(r, carry):
            peer = lax.rem(seq + r, 16)
            remote(
                loc.at[block(peer, HD), :], got.at[:, block(seq, ROWS)],
                in_send.at[n], in_recv.at[n], (peer, ctx),
            ).start()
            return carry

        lax.fori_loop(1, 16, one, 0)
        got[:, block(seq, ROWS)] = loc[block(seq, HD), :]

    def wait_in(n, loc, got):
        remote(
            loc.at[: 15 * HD, :], got.at[:, : 15 * ROWS],
            in_send.at[n], in_recv.at[n], (sibling, ctx),
        ).wait_recv()

    def send_rims(n, got):
        one = remote(rim_out.at[n, 0], got.at[1], rim_send.at[n, 0], rim_recv.at[n, 0], before_id)
        two = remote(rim_out.at[n, 1], got.at[0], rim_send.at[n, 1], rim_recv.at[n, 1], after_id)
        one.start()
        two.start()
        return one, two

    rim_out[0, 0] = x_ref[:16, :]
    rim_out[0, 1] = x_ref[ROWS - 16 :, :]
    turn(q_ref, q_loc)
    pl.semaphore_wait(barrier, 2 + 15 + 15 + 8)

    x_rims = send_rims(0, x_rim)
    send_in(0, q_loc, q_t)
    turn(k_ref, k_loc)
    send_in(1, k_loc, k_t)
    turn(v_ref, v_loc)
    send_in(2, v_loc, v_t)

    def widen(dst, start, src, factor=None):
        for c in range(GROUPS):
            piece = src[:, c * LANES : (c + 1) * LANES].astype(F32)
            dst[c, start : start + piece.shape[0], :] = piece if factor is None else piece * factor

    widen(x_pad, 16, x_ref)
    widen(go_wide, 0, go_ref)
    has_before = (place > 0).astype(F32)
    has_after = (place < total - 1).astype(F32)
    for rim in x_rims:
        rim.wait_recv()
    widen(x_pad, 0, x_rim.at[0], has_before)
    widen(x_pad, 16 + ROWS, x_rim.at[1], has_after)

    def rows(ref, p, c):
        return ref[c, pl.ds(p, 8, stride=16), :]

    def forward(c, carry):
        cs = block(c, LANES)
        xs = [rows(x_pad, p, c) for p in range(48)]
        acc = [jnp.zeros((8, LANES), F32) for _ in range(16)]
        for j in range(TAPS):
            tap = jnp.broadcast_to(taps_ref[j : j + 1, cs], (8, LANES))
            for i in range(16):
                acc[i] = acc[i] + tap * xs[i + j + 1]
        for i in range(16):
            pre = acc[i]
            sig = jax.nn.sigmoid(pre)
            slope = sig * (1.0 + pre * (1.0 - sig))
            grad = (rows(go_wide, i, c) * slope).astype(BF).astype(F32)
            g_pad[c, pl.ds(16 + i, 8, stride=16), :] = grad
        return carry

    lax.fori_loop(0, GROUPS, forward, 0)
    for c in range(GROUPS):
        s = slice(c * LANES, (c + 1) * LANES)
        rim_out[1, 0, :, s] = g_pad[c, 16:32, :].astype(BF)
        rim_out[1, 1, :, s] = g_pad[c, ROWS : ROWS + 16, :].astype(BF)
    g_rims = send_rims(1, g_rim)

    def tap_grads(c, carry):
        cs = block(c, LANES)
        xs = [rows(x_pad, p, c) for p in range(48)]
        acc = [jnp.zeros((8, LANES), F32) for _ in range(TAPS)]
        for i in range(16):
            grad = rows(g_pad, 16 + i, c)
            for j in range(TAPS):
                acc[j] = acc[j] + grad * xs[i + j + 1]
        for j in range(TAPS):
            part[j : j + 1, cs] = jnp.sum(acc[j], axis=0, keepdims=True)
        return carry

    lax.fori_loop(0, GROUPS, tap_grads, 0)
    sum_a = remote(
        part.at[block(1 - core, 16), :], pair_in, sum_send.at[0], sum_recv.at[0], (sibling, ctx)
    )
    sum_a.start()

    row_bit = lax.broadcasted_iota(jnp.int32, (32, HEADS), 0)
    planes = [
        lax.shift_right_logical(jnp.broadcast_to(bits_ref[w : w + 1, :], (32, HEADS)), row_bit) & 1
        for w in range(ROWS // 32)
    ]
    keep = (1 - jnp.concatenate(planes, axis=0)).astype(F32) * (4.0 / 3.0)
    keep = jnp.concatenate([keep, jnp.zeros((ROWS, LANES - HEADS), F32)], axis=1).T[:HEADS]
    frame = seq * ROWS + lax.broadcasted_iota(jnp.int32, (HEADS, ROWS), 1)
    keep_t[...] = keep * jnp.where(frame < length, 1.0, 0.0)

    for rim in g_rims:
        rim.wait_recv()
    widen(g_pad, 0, g_rim.at[0], has_before)
    widen(g_pad, 16 + ROWS, g_rim.at[1], has_after)

    def backward(c, carry):
        cs = block(c, LANES)
        gs = [rows(g_pad, p, c) for p in range(47)]
        acc = [rows(go_wide, i, c) for i in range(16)]
        for j in range(TAPS):
            tap = jnp.broadcast_to(taps_ref[j : j + 1, cs], (8, LANES))
            for i in range(16):
                acc[i] = acc[i] + tap * gs[i + 31 - j]
        for i in range(16):
            gi_wide[c, pl.ds(i, 8, stride=16), :] = acc[i]
        return carry

    lax.fori_loop(0, GROUPS, backward, 0)
    for j in range(GROUPS):
        s = slice(j * LANES, (j + 1) * LANES)
        wide = gi_wide[j]
        gb_ref[:, s] = wide.astype(BF)
        turned = wide.T
        for at in range(0, LANES, 32):
            head = (j * LANES + at) // HD
            piece = turned[at : at + 32] * keep_t[head : head + 1, :]
            a_loc[j * LANES + at : j * LANES + at + 32, :] = piece.astype(BF)
    send_in(3, a_loc, a_t)

    sum_a.wait_recv()
    mine = part[block(core, 16), :] + pair_in[...]
    for t in range(16):
        half[t] = mine[t : t + 1, :]

    def send_z(src, dst, n, whole):
        def one(r, carry):
            other = lax.rem(z + r, NZ)
            remote(
                src if whole else src.at[other], dst.at[z],
                sum_send.at[n], sum_recv.at[n], (seq, y_hi * NZ + other),
            ).start()
            return carry

        lax.fori_loop(1, NZ, one, 0)

    def wait_sum(n, buf):
        remote(
            buf.at[:15], buf.at[:15], sum_send.at[n], sum_recv.at[n], (sibling, ctx)
        ).wait_recv()

    send_z(half, z_in, 1, False)
    z_in[z] = half[z]

    tail_row = lax.broadcasted_iota(jnp.int32, (LANES - HD, LANES), 0)
    ones_row = jnp.where(tail_row == 0, 1.0, 0.0).astype(BF)
    zero_rows = jnp.zeros((LANES - HD, LANES), BF)

    def natural(dst, src, tail):
        for j in range(SEG // LANES):
            s = slice(j * LANES, (j + 1) * LANES)
            dst[s, :] = jnp.concatenate([src[:, s], tail], axis=0).T

    wait_in(0, q_loc, q_t)
    natural(q_n, q_t, ones_row)
    wait_in(1, k_loc, k_t)
    natural(k_n, k_t, zero_rows)
    k_aug[:HD, :] = k_t[...]
    bias_row = lax.broadcasted_iota(jnp.int32, (LANES - HD, SEG), 0)
    key = lax.broadcasted_iota(jnp.int32, (LANES - HD, SEG), 1)
    k_aug[HD:, :] = jnp.where((bias_row == 0) & (key >= length), -1e30, 0.0).astype(BF)
    v_aug[HD:, :] = jnp.zeros((LANES - HD, SEG), BF)

    def scores(i):
        queries = q_n[i * QB : (i + 1) * QB, :]
        top = None
        for k in range(NB):
            ks = slice(k * QB, (k + 1) * QB)
            s = dot(queries, k_aug[:, ks])
            work[i % 2, :, ks] = s
            for t in halves(s):
                top = t if top is None else jnp.maximum(top, t)
        return jnp.max(top, axis=1, keepdims=True)

    def softmax(i, top):
        r = slice(i * QB, (i + 1) * QB)
        count = None
        for k in range(NB):
            ks = slice(k * QB, (k + 1) * QB)
            p = jnp.exp2((work[i % 2, :, ks] - top) * EXP2_SCALE)
            prob[r, ks] = p.astype(BF)
            for t in halves(p):
                count = t if count is None else count + t
        inv_ref[r, :] = 1.0 / jnp.sum(count, axis=1, keepdims=True)

    top = scores(0)
    for i in range(NB):
        next_top = scores(i + 1) if i + 1 < NB else None
        softmax(i, top)
        top = next_top

    wait_sum(1, z_in)
    chip_sum = z_in[0]
    for t in range(1, NZ):
        chip_sum = chip_sum + z_in[t]
    chip_out[...] = chip_sum
    chip_in[here] = chip_sum

    def send_chip(r, carry):
        remote(
            chip_out, chip_in.at[here], sum_send.at[2], sum_recv.at[2], to_chip(r)
        ).start()
        return carry

    lax.fori_loop(1, 16, send_chip, 0)

    def send_out(n, src, dst, tile):
        for c in range(2):
            peer = tile * 2 + c

            @pl.when(peer != seq)
            def _():
                remote(
                    src.at[:, block(peer, ROWS)], dst.at[block(seq, HD), :],
                    out_send.at[n], out_recv.at[n], (peer, ctx),
                ).start()

    def keep_own(src, dst):
        dst[block(seq, HD), :] = src[:, block(seq, ROWS)]

    def wait_out(n, src, dst):
        remote(
            src.at[:, : 15 * ROWS], dst.at[: 15 * HD, :],
            out_send.at[n], out_recv.at[n], (sibling, ctx),
        ).wait_recv()

    def columns(n, left, right, src, dst):
        for i in range(NB):
            tile = lax.rem(chip + 1 + i, 8)
            src[:, block(tile, QB)] = dot(left[...], right[:, block(tile, QB)]).astype(BF)
            send_out(n, src, dst, tile)
        keep_own(src, dst)

    wait_in(2, v_loc, v_t)
    v_aug[:HD, :] = v_t[...]
    wait_in(3, a_loc, a_t)
    natural(a_n, a_t, zero_rows)
    for j in range(SEG // LANES):
        s = slice(j * LANES, (j + 1) * LANES)
        side[:, s] = (a_n[s, :].astype(F32) * inv_ref[s, :]).astype(BF).T[:HD]
    columns(2, side, prob, dv_t, dv_in)

    wait_sum(2, chip_in)
    full = chip_in[0]
    for t in range(1, 16):
        full = full + chip_in[t]
    full = full * (1.0 / 32.0)
    full_out[...] = full
    full_z[z] = full
    send_z(full_out, full_z, 3, True)

    def grad_probs(i):
        tile = lax.rem(chip + 1 + i, 8)
        r = block(tile, QB)
        grads = a_n[r, :]
        acc = None
        for k in range(NB):
            ks = slice(k * QB, (k + 1) * QB)
            g = dot(grads, v_aug[:, ks])
            work[i % 2, :, ks] = g
            for t in halves(g * prob[r, ks].astype(F32)):
                acc = t if acc is None else acc + t
        return acc

    def grad_scores(i, acc):
        tile = lax.rem(chip + 1 + i, 8)
        r = block(tile, QB)
        inverse = inv_ref[r, :]
        delta = jnp.sum(acc, axis=1, keepdims=True) * inverse
        for k in range(NB):
            ks = slice(k * QB, (k + 1) * QB)
            ds = prob[r, ks].astype(F32) * (work[i % 2, :, ks] - delta)
            dscore[r, ks] = ds.astype(BF)
        dq = (dot(dscore[r, :], k_n[...]) * (inverse * SCALE)).astype(BF)
        for j in range(QB // LANES):
            dq_t[:, block(tile * 2 + j, LANES)] = dq[j * LANES : (j + 1) * LANES, :].T[:HD]
        send_out(0, dq_t, dq_in, tile)

    acc = grad_probs(0)
    for i in range(NB):
        next_acc = grad_probs(i + 1) if i + 1 < NB else None
        grad_scores(i, acc)
        acc = next_acc
    keep_own(dq_t, dq_in)

    wait_sum(3, full_z)
    sum_e = remote(full_z, full_pair, sum_send.at[4], sum_recv.at[4], (sibling, ctx))
    sum_e.start()

    for j in range(SEG // LANES):
        s = slice(j * LANES, (j + 1) * LANES)
        side[:, s] = (q_n[s, :].astype(F32) * (inv_ref[s, :] * SCALE)).astype(BF).T[:HD]
    columns(1, side, dscore, dk_t, dk_in)

    sum_e.wait_recv()
    first = core == 0
    for t in range(16):
        own, got = full_z[t], full_pair[t]
        gk_ref[t : t + 1, :] = jnp.where(first, own, got)
        gk_ref[16 + t : 17 + t, :] = jnp.where(first, got, own)

    def turn_back(src, dst):
        for j in range(GROUPS):
            s = slice(j * LANES, (j + 1) * LANES)
            dst[:, s] = src[s, :].T

    wait_out(2, dv_t, dv_in)
    turn_back(dv_in, dv_ref)
    wait_out(0, dq_t, dq_in)
    turn_back(dq_in, dq_ref)
    wait_out(1, dk_t, dk_in)
    turn_back(dk_in, dk_ref)

    for n, (loc, got) in enumerate(((q_loc, q_t), (k_loc, k_t), (v_loc, v_t), (a_loc, a_t))):
        remote(
            loc.at[: 15 * HD, :], got.at[:, : 15 * ROWS],
            in_send.at[n], in_recv.at[n], (sibling, ctx),
        ).wait_send()
    for n, (src, dst) in enumerate(((dq_t, dq_in), (dk_t, dk_in), (dv_t, dv_in))):
        remote(
            src.at[:, : 15 * ROWS], dst.at[: 15 * HD, :],
            out_send.at[n], out_recv.at[n], (sibling, ctx),
        ).wait_send()
    for copy in (*x_rims, *g_rims, sum_a, sum_e):
        copy.wait_send()
    for n, buf in ((1, half), (2, chip_in), (3, full_z)):
        remote(
            buf.at[:15], buf.at[:15], sum_send.at[n], sum_recv.at[n], (sibling, ctx)
        ).wait_send()


def on_device(
    queries, key_rows, value_rows, block_in, grad_out, conv_kernel, drop_bits, seg_length
):
    vmem = pl.BlockSpec(memory_space=pltpu.VMEM)
    smem = pl.BlockSpec(memory_space=pltpu.SMEM)
    local = jax.ShapeDtypeStruct((ROWS, WIDTH), BF)
    dma = pltpu.SemaphoreType.DMA
    scratch = [
        pltpu.VMEM((GROUPS, ROWS + 32, LANES), F32),
        pltpu.VMEM((GROUPS, ROWS + 32, LANES), F32),
        pltpu.VMEM((GROUPS, ROWS, LANES), F32),
        pltpu.VMEM((GROUPS, ROWS, LANES), F32),
        pltpu.VMEM((2, 2, 16, WIDTH), BF),
        pltpu.VMEM((2, 16, WIDTH), BF),
        pltpu.VMEM((2, 16, WIDTH), BF),
        pltpu.VMEM((HEADS, ROWS), F32),
        pltpu.VMEM((TAPS, WIDTH), F32),
        pltpu.VMEM((16, WIDTH), F32),
        pltpu.VMEM((16, 1, WIDTH), F32),
        pltpu.VMEM((16, 1, WIDTH), F32),
        pltpu.VMEM((1, WIDTH), F32),
        pltpu.VMEM((16, 1, WIDTH), F32),
        pltpu.VMEM((1, WIDTH), F32),
        pltpu.VMEM((16, 1, WIDTH), F32),
        pltpu.VMEM((16, 1, WIDTH), F32),
        *[pltpu.VMEM((WIDTH, ROWS), BF) for _ in range(4)],
        *[pltpu.VMEM((HD, SEG), BF) for _ in range(4)],
        *[pltpu.VMEM((SEG, LANES), BF) for _ in range(3)],
        *[pltpu.VMEM((LANES, SEG), BF) for _ in range(2)],
        pltpu.VMEM((SEG, SEG), BF),
        pltpu.VMEM((SEG, SEG), BF),
        pltpu.VMEM((2, QB, SEG), F32),
        pltpu.VMEM((SEG, 1), F32),
        pltpu.VMEM((HD, SEG), BF),
        *[pltpu.VMEM((HD, SEG), BF) for _ in range(3)],
        *[pltpu.VMEM((WIDTH, ROWS), BF) for _ in range(3)],
        dma((4,)),
        dma((4,)),
        dma((3,)),
        dma((3,)),
        dma((2, 2)),
        dma((2, 2)),
        dma((5,)),
        dma((5,)),
    ]
    return pl.pallas_call(
        kernel,
        out_shape=(local, local, local, local, jax.ShapeDtypeStruct((TAPS, WIDTH), F32)),
        in_specs=[vmem] * 7 + [smem],
        out_specs=(vmem,) * 5,
        scratch_shapes=scratch,
        compiler_params=pltpu.CompilerParams(
            collective_id=0, has_side_effects=True, vmem_limit_bytes=56 * 1024 * 1024
        ),
        cost_estimate=pl.CostEstimate(
            flops=5 * 2 * SEG * SEG * HD, bytes_accessed=4 << 20, transcendentals=SEG * SEG
        ),
    )(queries, key_rows, value_rows, block_in, grad_out, conv_kernel, drop_bits, seg_length)


def solution(mesh):
    split = P(("ctx", "seq"), None)
    return jax.shard_map(
        on_device,
        mesh=mesh,
        in_specs=(split, split, split, split, split, P(), split, P("ctx")),
        out_specs=(split, split, split, split, P()),
        check_vma=False,
    )
```

```python
import functools
import math

import jax
import jax.numpy as jnp
from jax import lax
from jax.experimental import pallas as pl
from jax.experimental.pallas import tpu as pltpu
from jax.sharding import PartitionSpec as P

BF = jnp.bfloat16
F32 = jnp.float32
HD = 96
HEADS = 16
ROWS = 128
WIDTH = HEADS * HD
SEG = 2048
TAPS = 32
LANES = 128
GROUPS = WIDTH // LANES
QB = 256
NB = SEG // QB
NZ = 16
RIM = 16
STEPS = ((1, 2), (1, 1), (1, 3), (0, 2), (1, 0), (0, 1), (0, 3), (0, 0))
SCALE = 1.0 / math.sqrt(HD)
EXP2_SCALE = SCALE * math.log2(math.e)
MESH = pl.DeviceIdType.MESH


def dot(a, b):
    return lax.dot_general(a, b, (((1,), (0,)), ((), ())), preferred_element_type=F32)


def block(index, size):
    return pl.ds(pl.multiple_of(index * size, size), size)


def halves(x):
    return [x[:, c * LANES : (c + 1) * LANES] for c in range(x.shape[1] // LANES)]


def kernel(
    q_hbm, k_hbm, v_hbm, x_hbm, go_hbm, taps_hbm, bits_ref, len_ref,
    dq_in, dk_in, dv_in, gb_hbm, gk_ref,
    q_ref, k_ref, v_ref, x_ref, go_ref, taps_ref, gb_ref,
    x_pad, g_pad, go_wide, gi_wide, x_rim, go_rim, keep_t,
    part, pair_in, half, z_in, chip_out, chip_in, full_out, full_z, full_pair,
    q_loc, k_loc, v_loc, a_loc, q_t, k_t, v_t, a_t,
    q_n, k_n, a_n, k_aug, v_aug, prob, dscore, work, inv_ref, side,
    dq_t, dk_t, dv_t,
    in_send, in_recv, out_send, out_recv, rim_send, rim_recv, sum_send, sum_recv, load_sem, own_sem,
):
    seq = lax.axis_index("seq")
    ctx = lax.axis_index("ctx")
    chip = seq // 2
    core = seq % 2
    sibling = chip * 2 + (1 - core)
    y_hi = ctx // NZ
    z = ctx % NZ
    here = y_hi * 8 + chip
    place = ctx * 16 + seq
    total = 512
    before = lax.rem(place + total - 1, total)
    after = lax.rem(place + 1, total)
    before_id = (before % 16, before // 16)
    after_id = (after % 16, after // 16)
    length = len_ref[0]

    def remote(src, dst, send, recv, device):
        return pltpu.make_async_remote_copy(
            src_ref=src, dst_ref=dst, send_sem=send, recv_sem=recv,
            device_id=device, device_id_type=MESH,
        )

    def to_chip(r):
        other = lax.rem(here + r, 16)
        return ((other % 8) * 2 + core, (other // 8) * NZ + z)

    loads = [
        pltpu.make_async_copy(src, dst, load_sem.at[n])
        for n, (src, dst) in enumerate(
            (
                (q_hbm, q_ref), (x_hbm, x_ref), (go_hbm, go_ref),
                (k_hbm, k_ref), (v_hbm, v_ref), (taps_hbm, taps_ref),
            )
        )
    ]
    for load in loads:
        load.start()
    q_load, x_load, go_load, k_load, v_load, taps_load = loads

    barrier = pltpu.get_barrier_semaphore()

    def greet(device):
        pl.semaphore_signal(barrier, inc=1, device_id=device, device_id_type=MESH)

    greet(before_id)
    greet(after_id)

    def greet_some(r, carry):
        greet((lax.rem(seq + r, 16), ctx))
        greet((seq, y_hi * NZ + lax.rem(z + r, NZ)))
        return carry

    lax.fori_loop(1, 16, greet_some, 0)

    def greet_far(r, carry):
        greet((r * 2 + core, (1 - y_hi) * NZ + z))
        return carry

    lax.fori_loop(0, 8, greet_far, 0)

    def turn(src, dst):
        for j in range(GROUPS):
            s = slice(j * LANES, (j + 1) * LANES)
            dst[s, :] = src[:, s].T

    def send_in(n, loc, got):
        def one(r, carry):
            peer = lax.rem(seq + r, 16)
            remote(
                loc.at[block(peer, HD), :], got.at[:, block(seq, ROWS)],
                in_send.at[n], in_recv.at[n], (peer, ctx),
            ).start()
            return carry

        lax.fori_loop(1, 16, one, 0)
        got[:, block(seq, ROWS)] = loc[block(seq, HD), :]

    def wait_in(n, loc, got):
        remote(
            loc.at[: 15 * HD, :], got.at[:, : 15 * ROWS],
            in_send.at[n], in_recv.at[n], (sibling, ctx),
        ).wait_recv()

    q_load.wait()
    turn(q_ref, q_loc)
    x_load.wait()
    go_load.wait()
    pl.semaphore_wait(barrier, 2 + 15 + 15 + 8)

    rims = []
    for n, (src, got, size) in enumerate(((x_ref, x_rim, 2 * RIM), (go_ref, go_rim, RIM))):
        rims.append(
            remote(
                src.at[:size, :], got.at[1], rim_send.at[n, 0], rim_recv.at[n, 0], before_id
            )
        )
        rims.append(
            remote(
                src.at[ROWS - size :, :], got.at[0],
                rim_send.at[n, 1], rim_recv.at[n, 1], after_id,
            )
        )
    for rim in rims:
        rim.start()
    send_in(0, q_loc, q_t)
    k_load.wait()
    turn(k_ref, k_loc)
    send_in(1, k_loc, k_t)
    v_load.wait()
    turn(v_ref, v_loc)
    send_in(2, v_loc, v_t)

    def widen(dst, start, src, factor=None):
        for c in range(GROUPS):
            piece = src[:, c * LANES : (c + 1) * LANES].astype(F32)
            dst[c, start : start + piece.shape[0], :] = piece if factor is None else piece * factor

    widen(x_pad, 2 * RIM, x_ref)
    widen(go_wide, RIM, go_ref)
    has_before = (place > 0).astype(F32)
    has_after = (place < total - 1).astype(F32)
    taps_load.wait()
    for rim in rims:
        rim.wait_recv()
    widen(x_pad, 0, x_rim.at[0], has_before)
    widen(x_pad, 2 * RIM + ROWS, x_rim.at[1], has_after)
    widen(go_wide, 0, go_rim.at[0], has_before)
    widen(go_wide, RIM + ROWS, go_rim.at[1], has_after)

    def rows(ref, p, c, stride=16):
        return ref[c, pl.ds(p, 8, stride=stride), :]

    def forward(c, carry):
        cs = block(c, LANES)
        acc = [jnp.zeros((8, LANES), F32) for _ in range(20)]
        xs = [rows(x_pad, p, c, 20) for p in range(1, 52)]
        for j in range(TAPS):
            tap = jnp.broadcast_to(taps_ref[j : j + 1, cs], (8, LANES))
            for i in range(20):
                acc[i] = acc[i] + tap * xs[i + j]
        for i in range(20):
            pre = acc[i]
            sig = jax.nn.sigmoid(pre)
            slope = sig * (1.0 + pre * (1.0 - sig))
            grad = (rows(go_wide, i, c, 20) * slope).astype(BF).astype(F32)
            g_pad[c, pl.ds(i, 8, stride=20), :] = grad
        return carry

    lax.fori_loop(0, GROUPS, forward, 0)

    def backward(c, carry):
        cs = block(c, LANES)
        gs = [rows(g_pad, p, c) for p in range(47)]
        acc = [rows(go_wide, RIM + i, c) for i in range(16)]
        for j in range(TAPS):
            tap = jnp.broadcast_to(taps_ref[j : j + 1, cs], (8, LANES))
            for i in range(16):
                acc[i] = acc[i] + tap * gs[i + 31 - j]
        for i in range(16):
            gi_wide[c, pl.ds(i, 8, stride=16), :] = acc[i]
        return carry

    lax.fori_loop(0, GROUPS, backward, 0)

    row_bit = lax.broadcasted_iota(jnp.int32, (32, HEADS), 0)
    planes = [
        lax.shift_right_logical(jnp.broadcast_to(bits_ref[w : w + 1, :], (32, HEADS)), row_bit) & 1
        for w in range(ROWS // 32)
    ]
    keep = (1 - jnp.concatenate(planes, axis=0)).astype(F32) * (4.0 / 3.0)
    keep = jnp.concatenate([keep, jnp.zeros((ROWS, LANES - HEADS), F32)], axis=1).T[:HEADS]
    frame = seq * ROWS + lax.broadcasted_iota(jnp.int32, (HEADS, ROWS), 1)
    keep_t[...] = keep * jnp.where(frame < length, 1.0, 0.0)

    for j in range(GROUPS):
        s = slice(j * LANES, (j + 1) * LANES)
        wide = gi_wide[j]
        gb_ref[:, s] = wide.astype(BF)
        turned = wide.T
        for at in range(0, LANES, 32):
            head = (j * LANES + at) // HD
            piece = turned[at : at + 32] * keep_t[head : head + 1, :]
            a_loc[j * LANES + at : j * LANES + at + 32, :] = piece.astype(BF)
    send_in(3, a_loc, a_t)
    gb_store = pltpu.make_async_copy(gb_ref, gb_hbm, own_sem.at[3])
    gb_store.start()

    def tap_grads(c, carry):
        cs = block(c, LANES)
        xs = [rows(x_pad, p, c) for p in range(17, 64)]
        acc = [jnp.zeros((8, LANES), F32) for _ in range(TAPS)]
        for i in range(16):
            grad = rows(g_pad, RIM + i, c)
            for j in range(TAPS):
                acc[j] = acc[j] + grad * xs[i + j]
        for j in range(TAPS):
            part[j : j + 1, cs] = jnp.sum(acc[j], axis=0, keepdims=True)
        return carry

    lax.fori_loop(0, GROUPS, tap_grads, 0)
    sum_a = remote(
        part.at[block(1 - core, 16), :], pair_in, sum_send.at[0], sum_recv.at[0], (sibling, ctx)
    )
    sum_a.start()

    sum_a.wait_recv()
    mine = part[block(core, 16), :] + pair_in[...]
    for t in range(16):
        half[t] = mine[t : t + 1, :]

    def send_z(src, dst, n, whole):
        def one(r, carry):
            other = lax.rem(z + r, NZ)
            remote(
                src if whole else src.at[other], dst.at[z],
                sum_send.at[n], sum_recv.at[n], (seq, y_hi * NZ + other),
            ).start()
            return carry

        lax.fori_loop(1, NZ, one, 0)

    def wait_sum(n, buf):
        remote(
            buf.at[:15], buf.at[:15], sum_send.at[n], sum_recv.at[n], (sibling, ctx)
        ).wait_recv()

    send_z(half, z_in, 1, False)
    z_in[z] = half[z]

    tail_row = lax.broadcasted_iota(jnp.int32, (LANES - HD, LANES), 0)
    ones_row = jnp.where(tail_row == 0, 1.0, 0.0).astype(BF)
    zero_rows = jnp.zeros((LANES - HD, LANES), BF)

    def natural(dst, src, tail):
        for j in range(SEG // LANES):
            s = slice(j * LANES, (j + 1) * LANES)
            dst[s, :] = jnp.concatenate([src[:, s], tail], axis=0).T

    wait_in(0, q_loc, q_t)
    natural(q_n, q_t, ones_row)
    wait_in(1, k_loc, k_t)
    natural(k_n, k_t, zero_rows)
    k_aug[:HD, :] = k_t[...]
    bias_row = lax.broadcasted_iota(jnp.int32, (LANES - HD, SEG), 0)
    key = lax.broadcasted_iota(jnp.int32, (LANES - HD, SEG), 1)
    k_aug[HD:, :] = jnp.where((bias_row == 0) & (key >= length), -1e30, 0.0).astype(BF)
    v_aug[HD:, :] = jnp.zeros((LANES - HD, SEG), BF)

    def scores(i):
        queries = q_n[i * QB : (i + 1) * QB, :]
        top = None
        for k in range(NB):
            ks = slice(k * QB, (k + 1) * QB)
            s = dot(queries, k_aug[:, ks])
            work[i % 2, :, ks] = s
            for t in halves(s):
                top = t if top is None else jnp.maximum(top, t)
        return jnp.max(top, axis=1, keepdims=True)

    def softmax(i, top):
        r = slice(i * QB, (i + 1) * QB)
        count = None
        for k in range(NB):
            ks = slice(k * QB, (k + 1) * QB)
            p = jnp.exp2((work[i % 2, :, ks] - top) * EXP2_SCALE).astype(BF)
            prob[r, ks] = p
            for t in halves(p.astype(F32)):
                count = t if count is None else count + t
        inv_ref[r, :] = 1.0 / jnp.sum(count, axis=1, keepdims=True)

    top = scores(0)
    for i in range(NB):
        next_top = scores(i + 1) if i + 1 < NB else None
        softmax(i, top)
        top = next_top

    wait_sum(1, z_in)
    chip_sum = z_in[0]
    for t in range(1, NZ):
        chip_sum = chip_sum + z_in[t]
    chip_out[...] = chip_sum
    chip_in[here] = chip_sum

    def send_chip(r, carry):
        remote(
            chip_out, chip_in.at[here], sum_send.at[2], sum_recv.at[2], to_chip(r)
        ).start()
        return carry

    lax.fori_loop(1, 16, send_chip, 0)

    def send_out(n, src, dst, i):
        tile = tile_at(i)
        for peer in (tile * 2, tile * 2 + 1) if i < NB - 1 else (sibling,):
            remote(
                src.at[:, block(peer, ROWS)], dst.at[block(seq, HD), :],
                out_send.at[n], out_recv.at[n], (peer, ctx),
            ).start()

    def keep_own(n, src, dst):
        copy = pltpu.make_async_copy(
            src.at[:, block(seq, ROWS)], dst.at[block(seq, HD), :], own_sem.at[n]
        )
        copy.start()
        return copy

    def wait_out(n, src, dst):
        remote(
            src.at[:, : 15 * ROWS], dst.at[: 15 * HD, :],
            out_send.at[n], out_recv.at[n], (sibling, ctx),
        ).wait_recv()

    def tile_at(i):
        y, x = STEPS[i]
        return lax.rem(chip // 4 + y, 2) * 4 + lax.rem(chip % 4 + x, 4)

    def columns(n, left, right, src, dst):
        for i in range(NB):
            tile = tile_at(i)
            src[:, block(tile, QB)] = dot(left[...], right[:, block(tile, QB)]).astype(BF)
            send_out(n, src, dst, i)
        return keep_own(n, src, dst)

    wait_in(2, v_loc, v_t)
    v_aug[:HD, :] = v_t[...]
    wait_in(3, a_loc, a_t)
    natural(a_n, a_t, zero_rows)
    for j in range(SEG // LANES):
        s = slice(j * LANES, (j + 1) * LANES)
        side[:, s] = (a_n[s, :].astype(F32) * inv_ref[s, :]).astype(BF).T[:HD]
    dv_own = columns(2, side, prob, dv_t, dv_in)

    wait_sum(2, chip_in)
    full = chip_in[0]
    for t in range(1, 16):
        full = full + chip_in[t]
    full = full * (1.0 / 32.0)
    full_out[...] = full
    full_z[z] = full
    send_z(full_out, full_z, 3, True)

    def grad_probs(i):
        tile = tile_at(i)
        r = block(tile, QB)
        grads = a_n[r, :]
        acc = None
        for k in range(NB):
            ks = slice(k * QB, (k + 1) * QB)
            g = dot(grads, v_aug[:, ks])
            work[i % 2, :, ks] = g
            for t in halves(g * prob[r, ks].astype(F32)):
                acc = t if acc is None else acc + t
        return acc

    def grad_scores(i, acc):
        tile = tile_at(i)
        r = block(tile, QB)
        inverse = inv_ref[r, :]
        delta = jnp.sum(acc, axis=1, keepdims=True) * inverse
        for k in range(NB):
            ks = slice(k * QB, (k + 1) * QB)
            ds = prob[r, ks].astype(F32) * (work[i % 2, :, ks] - delta)
            dscore[r, ks] = ds.astype(BF)
        dq = (dot(dscore[r, :], k_n[...]) * (inverse * SCALE)).astype(BF)
        for j in range(QB // LANES):
            dq_t[:, block(tile * 2 + j, LANES)] = dq[j * LANES : (j + 1) * LANES, :].T[:HD]
        send_out(0, dq_t, dq_in, i)

    acc = grad_probs(0)
    for i in range(NB):
        next_acc = grad_probs(i + 1) if i + 1 < NB else None
        grad_scores(i, acc)
        acc = next_acc
    dq_own = keep_own(0, dq_t, dq_in)

    wait_sum(3, full_z)
    sum_e = remote(full_z, full_pair, sum_send.at[4], sum_recv.at[4], (sibling, ctx))
    sum_e.start()

    for j in range(SEG // LANES):
        s = slice(j * LANES, (j + 1) * LANES)
        side[:, s] = (q_n[s, :].astype(F32) * (inv_ref[s, :] * SCALE)).astype(BF).T[:HD]
    dk_own = columns(1, side, dscore, dk_t, dk_in)

    sum_e.wait_recv()
    first = core == 0
    for t in range(16):
        own, got = full_z[t], full_pair[t]
        gk_ref[t : t + 1, :] = jnp.where(first, own, got)
        gk_ref[16 + t : 17 + t, :] = jnp.where(first, got, own)

    for n, (src, dst) in enumerate(((dq_t, dq_in), (dk_t, dk_in), (dv_t, dv_in))):
        wait_out(n, src, dst)
    for copy in (dq_own, dk_own, dv_own, gb_store):
        copy.wait()

    for n, (loc, got) in enumerate(((q_loc, q_t), (k_loc, k_t), (v_loc, v_t), (a_loc, a_t))):
        remote(
            loc.at[: 15 * HD, :], got.at[:, : 15 * ROWS],
            in_send.at[n], in_recv.at[n], (sibling, ctx),
        ).wait_send()
    for n, (src, dst) in enumerate(((dq_t, dq_in), (dk_t, dk_in), (dv_t, dv_in))):
        remote(
            src.at[:, : 15 * ROWS], dst.at[: 15 * HD, :],
            out_send.at[n], out_recv.at[n], (sibling, ctx),
        ).wait_send()
    for copy in (*rims, sum_a, sum_e):
        copy.wait_send()
    for n, buf in ((1, half), (2, chip_in), (3, full_z)):
        remote(
            buf.at[:15], buf.at[:15], sum_send.at[n], sum_recv.at[n], (sibling, ctx)
        ).wait_send()


def on_device(
    queries, key_rows, value_rows, block_in, grad_out, conv_kernel, drop_bits, seg_length
):
    vmem = pl.BlockSpec(memory_space=pltpu.VMEM)
    smem = pl.BlockSpec(memory_space=pltpu.SMEM)
    local = jax.ShapeDtypeStruct((ROWS, WIDTH), BF)
    dma = pltpu.SemaphoreType.DMA
    scratch = [
        *[pltpu.VMEM((ROWS, WIDTH), BF) for _ in range(5)],
        pltpu.VMEM((TAPS, WIDTH), F32),
        pltpu.VMEM((ROWS, WIDTH), BF),
        pltpu.VMEM((GROUPS, ROWS + 4 * RIM, LANES), F32),
        pltpu.VMEM((GROUPS, ROWS + 2 * RIM, LANES), F32),
        pltpu.VMEM((GROUPS, ROWS + 2 * RIM, LANES), F32),
        pltpu.VMEM((GROUPS, ROWS, LANES), F32),
        pltpu.VMEM((2, 2 * RIM, WIDTH), BF),
        pltpu.VMEM((2, RIM, WIDTH), BF),
        pltpu.VMEM((HEADS, ROWS), F32),
        pltpu.VMEM((TAPS, WIDTH), F32),
        pltpu.VMEM((16, WIDTH), F32),
        pltpu.VMEM((16, 1, WIDTH), F32),
        pltpu.VMEM((16, 1, WIDTH), F32),
        pltpu.VMEM((1, WIDTH), F32),
        pltpu.VMEM((16, 1, WIDTH), F32),
        pltpu.VMEM((1, WIDTH), F32),
        pltpu.VMEM((16, 1, WIDTH), F32),
        pltpu.VMEM((16, 1, WIDTH), F32),
        *[pltpu.VMEM((WIDTH, ROWS), BF) for _ in range(4)],
        *[pltpu.VMEM((HD, SEG), BF) for _ in range(4)],
        *[pltpu.VMEM((SEG, LANES), BF) for _ in range(3)],
        *[pltpu.VMEM((LANES, SEG), BF) for _ in range(2)],
        pltpu.VMEM((SEG, SEG), BF),
        pltpu.VMEM((SEG, SEG), BF),
        pltpu.VMEM((2, QB, SEG), F32),
        pltpu.VMEM((SEG, 1), F32),
        pltpu.VMEM((HD, SEG), BF),
        *[pltpu.VMEM((HD, SEG), BF) for _ in range(3)],
        dma((4,)),
        dma((4,)),
        dma((3,)),
        dma((3,)),
        dma((2, 2)),
        dma((2, 2)),
        dma((5,)),
        dma((5,)),
        dma((6,)),
        dma((4,)),
    ]
    hbm = pl.BlockSpec(memory_space=pl.ANY)
    turned = jax.ShapeDtypeStruct((WIDTH, ROWS), BF)
    taps_out = jax.ShapeDtypeStruct((TAPS, WIDTH), F32)
    dq, dk, dv, gb, gk = pl.pallas_call(
        kernel,
        out_shape=(turned, turned, turned, local, taps_out),
        in_specs=[hbm] * 6 + [vmem, smem],
        out_specs=(hbm,) * 4 + (vmem,),
        scratch_shapes=scratch,
        compiler_params=pltpu.CompilerParams(
            collective_id=0, has_side_effects=True, vmem_limit_bytes=56 * 1024 * 1024
        ),
        cost_estimate=pl.CostEstimate(
            flops=5 * 2 * SEG * SEG * HD, bytes_accessed=4 << 20, transcendentals=SEG * SEG
        ),
    )(queries, key_rows, value_rows, block_in, grad_out, conv_kernel, drop_bits, seg_length)

    def finish(dq_i, dk_i, dv_i, gb_i, gk_i, dq_o, dk_o, dv_o, gb_o, gk_o):
        for src, dst in ((dq_i, dq_o), (dk_i, dk_o), (dv_i, dv_o)):
            for j in range(dst.shape[1] // LANES):
                s = slice(j * LANES, (j + 1) * LANES)
                dst[:, s] = src[s, :].T
        gb_o[...] = gb_i[...]
        gk_o[...] = gk_i[...]

    wide = 4 * HD
    by_rows = pl.BlockSpec((wide, ROWS), lambda i: (i, 0))
    by_columns = pl.BlockSpec((ROWS, wide), lambda i: (0, i))
    taps_columns = pl.BlockSpec((TAPS, wide), lambda i: (0, i))
    return pl.pallas_call(
        finish,
        grid=(WIDTH // wide,),
        out_shape=(local, local, local, local, taps_out),
        in_specs=[by_rows] * 3 + [by_columns, taps_columns],
        out_specs=[by_columns] * 4 + [taps_columns],
    )(dq, dk, dv, gb, gk)


def solution(mesh):
    split = P(("ctx", "seq"), None)
    return jax.shard_map(
        on_device,
        mesh=mesh,
        in_specs=(split, split, split, split, split, P(), split, P("ctx")),
        out_specs=(split, split, split, split, P()),
        check_vma=False,
    )
```

```python
import functools
import math

import jax
import jax.numpy as jnp
from jax import lax
from jax.experimental import pallas as pl
from jax.experimental.pallas import tpu as pltpu
from jax.sharding import PartitionSpec as P

BF = jnp.bfloat16
F32 = jnp.float32
HD = 96
HEADS = 16
ROWS = 128
WIDTH = HEADS * HD
SEG = 2048
TAPS = 32
LANES = 128
GROUPS = WIDTH // LANES
QB = 256
NB = SEG // QB
NZ = 16
RIM = 16
STEPS = ((1, 2), (1, 1), (1, 3), (0, 2), (1, 0), (0, 1), (0, 3), (0, 0))
BACK = tuple(STEPS.index((-y % 2, -x % 4)) for y, x in STEPS)
OWN = 2 * (len(STEPS) - 1)
SCALE = 1.0 / math.sqrt(HD)
EXP2_SCALE = SCALE * math.log2(math.e)
MESH = pl.DeviceIdType.MESH


def dot(a, b):
    return lax.dot_general(a, b, (((1,), (0,)), ((), ())), preferred_element_type=F32)


def block(index, size):
    if isinstance(index, int):
        return pl.ds(index * size, size)
    return pl.ds(pl.multiple_of(index * size, size), size)


def halves(x):
    return [x[:, c * LANES : (c + 1) * LANES] for c in range(x.shape[1] // LANES)]


def kernel(
    q_hbm, k_hbm, v_hbm, x_hbm, go_hbm, taps_hbm, bits_hbm, len_ref,
    dq_in, dk_in, dv_in, gb_hbm, gk_ref,
    q_ref, k_ref, v_ref, x_ref, go_ref, taps_ref, bits_ref, gb_ref,
    x_pad, g_pad, go_wide, gi_wide, x_rim, go_rim, keep_t,
    part, pair_in, half, z_in, x_out, x_in, y_out, y_in, full_out, full_z, full_pair,
    q_loc, k_loc, v_loc, a_loc, q_t, k_t, v_t, a_t,
    q_n, k_n, a_n, k_aug, v_aug, prob, dscore, work, inv_ref, side, q_side,
    dq_t, dk_t, dv_t,
    in_send, in_recv, out_send, out_recv, rim_send, rim_recv, sum_send, sum_recv, load_sem, own_sem,
):
    seq = lax.axis_index("seq")
    ctx = lax.axis_index("ctx")
    chip = seq // 2
    core = seq % 2
    sibling = chip * 2 + (1 - core)
    y_hi = ctx // NZ
    z = ctx % NZ
    at_x = chip % 4
    at_y = y_hi * 2 + chip // 4
    place = ctx * 16 + seq
    total = 512
    before = lax.rem(place + total - 1, total)
    after = lax.rem(place + 1, total)
    before_id = (before % 16, before // 16)
    after_id = (after % 16, after // 16)
    length = len_ref[0]

    def remote(src, dst, send, recv, device):
        return pltpu.make_async_remote_copy(
            src_ref=src, dst_ref=dst, send_sem=send, recv_sem=recv,
            device_id=device, device_id_type=MESH,
        )

    loads = [
        pltpu.make_async_copy(src, dst, load_sem.at[n])
        for n, (src, dst) in enumerate(
            (
                (q_hbm, q_ref), (x_hbm, x_ref), (go_hbm, go_ref),
                (k_hbm, k_ref), (v_hbm, v_ref), (taps_hbm, taps_ref),
                (bits_hbm, bits_ref),
            )
        )
    ]
    for load in loads:
        load.start()
    q_load, x_load, go_load, k_load, v_load, taps_load, bits_load = loads

    barrier = pltpu.get_barrier_semaphore()

    def greet(device):
        pl.semaphore_signal(barrier, inc=1, device_id=device, device_id_type=MESH)

    greet(before_id)
    greet(after_id)

    def greet_some(r, carry):
        greet((lax.rem(seq + r, 16), ctx))
        greet((seq, y_hi * NZ + lax.rem(z + r, NZ)))
        return carry

    lax.fori_loop(1, 16, greet_some, 0)

    for low in range(2):
        greet(((low * 4 + at_x) * 2 + core, (1 - y_hi) * NZ + z))

    def turn(src, dst):
        for j in range(GROUPS):
            s = slice(j * LANES, (j + 1) * LANES)
            dst[s, :] = src[:, s].T

    def tile_at(i):
        y, x = STEPS[i]
        return lax.rem(chip // 4 + y, 2) * 4 + lax.rem(chip % 4 + x, 4)

    def peers_at(i):
        tile = tile_at(i)
        return (tile * 2, tile * 2 + 1) if i < NB - 1 else (sibling,)

    def send_in(n, loc, got):
        for i in range(NB):
            for peer in peers_at(i):
                remote(
                    loc.at[block(peer, HD), :], got.at[:, block(2 * BACK[i] + core, ROWS)],
                    in_send.at[n], in_recv.at[n], (peer, ctx),
                ).start()
        got[:, block(OWN + core, ROWS)] = loc[block(seq, HD), :]

    def wait_in(n, loc, got):
        remote(
            loc.at[: 15 * HD, :], got.at[:, : 15 * ROWS],
            in_send.at[n], in_recv.at[n], (sibling, ctx),
        ).wait_recv()

    q_load.wait()
    turn(q_ref, q_loc)
    x_load.wait()
    go_load.wait()
    pl.semaphore_wait(barrier, 2 + 15 + 15 + 2)

    rims = []
    for n, (src, got, size) in enumerate(((x_ref, x_rim, 2 * RIM), (go_ref, go_rim, RIM))):
        rims.append(
            remote(
                src.at[:size, :], got.at[1], rim_send.at[n, 0], rim_recv.at[n, 0], before_id
            )
        )
        rims.append(
            remote(
                src.at[ROWS - size :, :], got.at[0],
                rim_send.at[n, 1], rim_recv.at[n, 1], after_id,
            )
        )
    for rim in rims:
        rim.start()
    send_in(0, q_loc, q_t)
    k_load.wait()
    turn(k_ref, k_loc)
    send_in(1, k_loc, k_t)
    v_load.wait()
    turn(v_ref, v_loc)
    send_in(2, v_loc, v_t)

    def widen(dst, start, src, factor=None):
        for c in range(GROUPS):
            piece = src[:, c * LANES : (c + 1) * LANES].astype(F32)
            dst[c, start : start + piece.shape[0], :] = piece if factor is None else piece * factor

    widen(x_pad, 2 * RIM, x_ref)
    widen(go_wide, RIM, go_ref)
    has_before = (place > 0).astype(F32)
    has_after = (place < total - 1).astype(F32)
    taps_load.wait()
    bits_load.wait()
    for rim in rims:
        rim.wait_recv()
    widen(x_pad, 0, x_rim.at[0], has_before)
    widen(x_pad, 2 * RIM + ROWS, x_rim.at[1], has_after)
    widen(go_wide, 0, go_rim.at[0], has_before)
    widen(go_wide, RIM + ROWS, go_rim.at[1], has_after)

    def rows(ref, p, c, stride=16):
        return ref[c, pl.ds(p, 8, stride=stride), :]

    def forward(c, carry):
        cs = block(c, LANES)
        acc = [jnp.zeros((8, LANES), F32) for _ in range(20)]
        xs = [rows(x_pad, p, c, 20) for p in range(1, 52)]
        for j in range(TAPS):
            tap = jnp.broadcast_to(taps_ref[j : j + 1, cs], (8, LANES))
            for i in range(20):
                acc[i] = acc[i] + tap * xs[i + j]
        for i in range(20):
            pre = acc[i]
            sig = jax.nn.sigmoid(pre)
            slope = sig * (1.0 + pre * (1.0 - sig))
            grad = (rows(go_wide, i, c, 20) * slope).astype(BF).astype(F32)
            g_pad[c, pl.ds(i, 8, stride=20), :] = grad
        return carry

    lax.fori_loop(0, GROUPS, forward, 0)

    def backward(c, carry):
        cs = block(c, LANES)
        gs = [rows(g_pad, p, c) for p in range(47)]
        acc = [rows(go_wide, RIM + i, c) for i in range(16)]
        for j in range(TAPS):
            tap = jnp.broadcast_to(taps_ref[j : j + 1, cs], (8, LANES))
            for i in range(16):
                acc[i] = acc[i] + tap * gs[i + 31 - j]
        for i in range(16):
            gi_wide[c, pl.ds(i, 8, stride=16), :] = acc[i]
        return carry

    lax.fori_loop(0, GROUPS, backward, 0)

    row_bit = lax.broadcasted_iota(jnp.int32, (32, HEADS), 0)
    planes = [
        lax.shift_right_logical(jnp.broadcast_to(bits_ref[w : w + 1, :], (32, HEADS)), row_bit) & 1
        for w in range(ROWS // 32)
    ]
    keep = (1 - jnp.concatenate(planes, axis=0)).astype(F32) * (4.0 / 3.0)
    keep = jnp.concatenate([keep, jnp.zeros((ROWS, LANES - HEADS), F32)], axis=1).T[:HEADS]
    frame = seq * ROWS + lax.broadcasted_iota(jnp.int32, (HEADS, ROWS), 1)
    keep_t[...] = keep * jnp.where(frame < length, 1.0, 0.0)

    for j in range(GROUPS):
        s = slice(j * LANES, (j + 1) * LANES)
        wide = gi_wide[j]
        gb_ref[:, s] = wide.astype(BF)
        turned = wide.T
        for at in range(0, LANES, 32):
            head = (j * LANES + at) // HD
            piece = turned[at : at + 32] * keep_t[head : head + 1, :]
            a_loc[j * LANES + at : j * LANES + at + 32, :] = piece.astype(BF)
    send_in(3, a_loc, a_t)
    gb_store = pltpu.make_async_copy(gb_ref, gb_hbm, own_sem.at[3])
    gb_store.start()

    def tap_grads(c, carry):
        cs = block(c, LANES)
        xs = [rows(x_pad, p, c) for p in range(17, 64)]
        acc = [jnp.zeros((8, LANES), F32) for _ in range(TAPS)]
        for i in range(16):
            grad = rows(g_pad, RIM + i, c)
            for j in range(TAPS):
                acc[j] = acc[j] + grad * xs[i + j]
        for j in range(TAPS):
            part[j : j + 1, cs] = jnp.sum(acc[j], axis=0, keepdims=True)
        return carry

    lax.fori_loop(0, GROUPS, tap_grads, 0)
    sum_a = remote(
        part.at[block(1 - core, 16), :], pair_in, sum_send.at[0], sum_recv.at[0], (sibling, ctx)
    )
    sum_a.start()

    sum_a.wait_recv()
    mine = part[block(core, 16), :] + pair_in[...]
    for t in range(16):
        half[t] = mine[t : t + 1, :]

    def send_z(src, dst, n, whole):
        def one(r, carry):
            other = lax.rem(z + r, NZ)
            remote(
                src if whole else src.at[other], dst.at[z],
                sum_send.at[n], sum_recv.at[n], (seq, y_hi * NZ + other),
            ).start()
            return carry

        lax.fori_loop(1, NZ, one, 0)

    def wait_sum(n, buf):
        others = buf.at[: buf.shape[0] - 1]
        remote(others, others, sum_send.at[n], sum_recv.at[n], (sibling, ctx)).wait_recv()

    send_z(half, z_in, 1, False)
    z_in[z] = half[z]

    tail_row = lax.broadcasted_iota(jnp.int32, (LANES - HD, LANES), 0)
    ones_row = jnp.where(tail_row == 0, 1.0, 0.0).astype(BF)
    zero_rows = jnp.zeros((LANES - HD, LANES), BF)

    def natural(dst, src, tail):
        for j in range(SEG // LANES):
            s = slice(j * LANES, (j + 1) * LANES)
            dst[s, :] = jnp.concatenate([src[:, s], tail], axis=0).T

    wait_in(0, q_loc, q_t)
    natural(q_n, q_t, ones_row)
    wait_in(1, k_loc, k_t)
    natural(k_n, k_t, zero_rows)
    k_aug[:HD, :] = k_t[...]
    bias_row = lax.broadcasted_iota(jnp.int32, (LANES - HD, QB), 0)
    lane = lax.broadcasted_iota(jnp.int32, (LANES - HD, QB), 1)
    for i in range(NB):
        dead = (bias_row == 0) & (tile_at(i) * QB + lane >= length)
        k_aug[HD:, i * QB : (i + 1) * QB] = jnp.where(dead, -1e30, 0.0).astype(BF)
    v_aug[HD:, :] = jnp.zeros((LANES - HD, SEG), BF)

    def scores(i):
        queries = q_n[i * QB : (i + 1) * QB, :]
        top = None
        for k in range(NB):
            ks = slice(k * QB, (k + 1) * QB)
            s = dot(queries, k_aug[:, ks])
            work[i % 2, :, ks] = s
            for t in halves(s):
                top = t if top is None else jnp.maximum(top, t)
        return jnp.max(top, axis=1, keepdims=True)

    def softmax(i, top):
        r = slice(i * QB, (i + 1) * QB)
        count = None
        for k in range(NB):
            ks = slice(k * QB, (k + 1) * QB)
            p = jnp.exp2((work[i % 2, :, ks] - top) * EXP2_SCALE).astype(BF)
            prob[r, ks] = p
            for t in halves(p.astype(F32)):
                count = t if count is None else count + t
        inv_ref[r, :] = 1.0 / jnp.sum(count, axis=1, keepdims=True)

    top = scores(0)
    for i in range(NB):
        next_top = scores(i + 1) if i + 1 < NB else None
        softmax(i, top)
        top = next_top

    for j in range(SEG // LANES):
        s = slice(j * LANES, (j + 1) * LANES)
        q_side[:, s] = (q_n[s, :].astype(F32) * (inv_ref[s, :] * SCALE)).astype(BF).T[:HD]

    def add_up(buf):
        value = buf[0]
        for t in range(1, buf.shape[0]):
            value = value + buf[t]
        return value

    wait_sum(1, z_in)
    x_out[...] = add_up(z_in)
    x_in[at_x] = x_out[...]
    for r in range(1, 4):
        other = (chip // 4) * 4 + lax.rem(at_x + r, 4)
        remote(
            x_out, x_in.at[at_x], sum_send.at[2], sum_recv.at[2], (other * 2 + core, ctx)
        ).start()

    def send_out(n, src, dst, i):
        for c, peer in enumerate(peers_at(i)):
            at = 2 * i + c if i < NB - 1 else OWN + 1 - core
            remote(
                src.at[:, block(at, ROWS)], dst.at[block(seq, HD), :],
                out_send.at[n], out_recv.at[n], (peer, ctx),
            ).start()

    def keep_own(n, src, dst):
        copy = pltpu.make_async_copy(
            src.at[:, block(OWN + core, ROWS)], dst.at[block(seq, HD), :], own_sem.at[n]
        )
        copy.start()
        return copy

    def wait_out(n, src, dst):
        remote(
            src.at[:, : 15 * ROWS], dst.at[: 15 * HD, :],
            out_send.at[n], out_recv.at[n], (sibling, ctx),
        ).wait_recv()

    def columns(n, left, right, src, dst):
        for i in range(NB):
            s = slice(i * QB, (i + 1) * QB)
            src[:, s] = dot(left[...], right[:, s]).astype(BF)
            send_out(n, src, dst, i)
        return keep_own(n, src, dst)

    wait_in(2, v_loc, v_t)
    v_aug[:HD, :] = v_t[...]
    wait_in(3, a_loc, a_t)
    natural(a_n, a_t, zero_rows)
    for j in range(SEG // LANES):
        s = slice(j * LANES, (j + 1) * LANES)
        side[:, s] = (a_n[s, :].astype(F32) * inv_ref[s, :]).astype(BF).T[:HD]
    dv_own = columns(2, side, prob, dv_t, dv_in)

    wait_sum(2, x_in)
    y_out[...] = add_up(x_in)
    y_in[at_y] = y_out[...]
    for r in range(1, 4):
        other = lax.rem(at_y + r, 4)
        remote(
            y_out, y_in.at[at_y], sum_send.at[5], sum_recv.at[5],
            (((other % 2) * 4 + at_x) * 2 + core, (other // 2) * NZ + z),
        ).start()

    def sum_back():
        wait_sum(5, y_in)
        full_out[...] = add_up(y_in) * (1.0 / 32.0)
        full_z[z] = full_out[...]
        send_z(full_out, full_z, 3, True)

    def grad_probs(i):
        r = slice(i * QB, (i + 1) * QB)
        grads = a_n[r, :]
        acc = None
        for k in range(NB):
            ks = slice(k * QB, (k + 1) * QB)
            g = dot(grads, v_aug[:, ks])
            work[i % 2, :, ks] = g
            for t in halves(g * prob[r, ks].astype(F32)):
                acc = t if acc is None else acc + t
        return acc

    def grad_scores(i, acc):
        r = slice(i * QB, (i + 1) * QB)
        inverse = inv_ref[r, :]
        delta = jnp.sum(acc, axis=1, keepdims=True) * inverse
        for k in range(NB):
            ks = slice(k * QB, (k + 1) * QB)
            ds = prob[r, ks].astype(F32) * (work[i % 2, :, ks] - delta)
            dscore[r, ks] = ds.astype(BF)
        dq = (dot(dscore[r, :], k_n[...]) * (inverse * SCALE)).astype(BF)
        for j in range(QB // LANES):
            dq_t[:, i * QB + j * LANES : i * QB + (j + 1) * LANES] = dq[j * LANES : (j + 1) * LANES, :].T[:HD]
        send_out(0, dq_t, dq_in, i)

    acc = grad_probs(0)
    for i in range(NB):
        next_acc = grad_probs(i + 1) if i + 1 < NB else None
        grad_scores(i, acc)
        acc = next_acc
        if i == NB // 2:
            sum_back()
    dq_own = keep_own(0, dq_t, dq_in)

    wait_sum(3, full_z)
    sum_e = remote(full_z, full_pair, sum_send.at[4], sum_recv.at[4], (sibling, ctx))
    sum_e.start()

    dk_own = columns(1, q_side, dscore, dk_t, dk_in)

    sum_e.wait_recv()
    first = core == 0
    for t in range(16):
        own, got = full_z[t], full_pair[t]
        gk_ref[t : t + 1, :] = jnp.where(first, own, got)
        gk_ref[16 + t : 17 + t, :] = jnp.where(first, got, own)

    for n, (src, dst) in enumerate(((dq_t, dq_in), (dk_t, dk_in), (dv_t, dv_in))):
        wait_out(n, src, dst)
    for copy in (dq_own, dk_own, dv_own, gb_store):
        copy.wait()

    for n, (loc, got) in enumerate(((q_loc, q_t), (k_loc, k_t), (v_loc, v_t), (a_loc, a_t))):
        remote(
            loc.at[: 15 * HD, :], got.at[:, : 15 * ROWS],
            in_send.at[n], in_recv.at[n], (sibling, ctx),
        ).wait_send()
    for n, (src, dst) in enumerate(((dq_t, dq_in), (dk_t, dk_in), (dv_t, dv_in))):
        remote(
            src.at[:, : 15 * ROWS], dst.at[: 15 * HD, :],
            out_send.at[n], out_recv.at[n], (sibling, ctx),
        ).wait_send()
    for copy in (*rims, sum_a, sum_e):
        copy.wait_send()
    for n, buf in ((1, z_in), (2, x_in), (5, y_in), (3, full_z)):
        others = buf.at[: buf.shape[0] - 1]
        remote(others, others, sum_send.at[n], sum_recv.at[n], (sibling, ctx)).wait_send()


def on_device(
    queries, key_rows, value_rows, block_in, grad_out, conv_kernel, drop_bits, seg_length
):
    vmem = pl.BlockSpec(memory_space=pltpu.VMEM)
    smem = pl.BlockSpec(memory_space=pltpu.SMEM)
    local = jax.ShapeDtypeStruct((ROWS, WIDTH), BF)
    dma = pltpu.SemaphoreType.DMA
    scratch = [
        *[pltpu.VMEM((ROWS, WIDTH), BF) for _ in range(5)],
        pltpu.VMEM((TAPS, WIDTH), F32),
        pltpu.VMEM((ROWS // 32, HEADS), jnp.int32),
        pltpu.VMEM((ROWS, WIDTH), BF),
        pltpu.VMEM((GROUPS, ROWS + 4 * RIM, LANES), F32),
        pltpu.VMEM((GROUPS, ROWS + 2 * RIM, LANES), F32),
        pltpu.VMEM((GROUPS, ROWS + 2 * RIM, LANES), F32),
        pltpu.VMEM((GROUPS, ROWS, LANES), F32),
        pltpu.VMEM((2, 2 * RIM, WIDTH), BF),
        pltpu.VMEM((2, RIM, WIDTH), BF),
        pltpu.VMEM((HEADS, ROWS), F32),
        pltpu.VMEM((TAPS, WIDTH), F32),
        pltpu.VMEM((16, WIDTH), F32),
        pltpu.VMEM((16, 1, WIDTH), F32),
        pltpu.VMEM((16, 1, WIDTH), F32),
        pltpu.VMEM((1, WIDTH), F32),
        pltpu.VMEM((4, 1, WIDTH), F32),
        pltpu.VMEM((1, WIDTH), F32),
        pltpu.VMEM((4, 1, WIDTH), F32),
        pltpu.VMEM((1, WIDTH), F32),
        pltpu.VMEM((16, 1, WIDTH), F32),
        pltpu.VMEM((16, 1, WIDTH), F32),
        *[pltpu.VMEM((WIDTH, ROWS), BF) for _ in range(4)],
        *[pltpu.VMEM((HD, SEG), BF) for _ in range(4)],
        *[pltpu.VMEM((SEG, LANES), BF) for _ in range(3)],
        *[pltpu.VMEM((LANES, SEG), BF) for _ in range(2)],
        pltpu.VMEM((SEG, SEG), BF),
        pltpu.VMEM((SEG, SEG), BF),
        pltpu.VMEM((2, QB, SEG), F32),
        pltpu.VMEM((SEG, 1), F32),
        pltpu.VMEM((HD, SEG), BF),
        pltpu.VMEM((HD, SEG), BF),
        *[pltpu.VMEM((HD, SEG), BF) for _ in range(3)],
        dma((4,)),
        dma((4,)),
        dma((3,)),
        dma((3,)),
        dma((2, 2)),
        dma((2, 2)),
        dma((6,)),
        dma((6,)),
        dma((7,)),
        dma((4,)),
    ]
    hbm = pl.BlockSpec(memory_space=pl.ANY)
    turned = jax.ShapeDtypeStruct((WIDTH, ROWS), BF)
    taps_out = jax.ShapeDtypeStruct((TAPS, WIDTH), F32)
    dq, dk, dv, gb, gk = pl.pallas_call(
        kernel,
        out_shape=(turned, turned, turned, local, taps_out),
        in_specs=[hbm] * 7 + [smem],
        out_specs=(hbm,) * 4 + (vmem,),
        scratch_shapes=scratch,
        compiler_params=pltpu.CompilerParams(
            collective_id=0, has_side_effects=True, vmem_limit_bytes=56 * 1024 * 1024
        ),
        cost_estimate=pl.CostEstimate(
            flops=5 * 2 * SEG * SEG * HD, bytes_accessed=4 << 20, transcendentals=SEG * SEG
        ),
    )(queries, key_rows, value_rows, block_in, grad_out, conv_kernel, drop_bits, seg_length)

    def finish(dq_i, dk_i, dv_i, gb_i, gk_i, dq_o, dk_o, dv_o, gb_o, gk_o):
        for src, dst in ((dq_i, dq_o), (dk_i, dk_o), (dv_i, dv_o)):
            for j in range(dst.shape[1] // LANES):
                s = slice(j * LANES, (j + 1) * LANES)
                dst[:, s] = src[s, :].T
        gb_o[...] = gb_i[...]
        gk_o[...] = gk_i[...]

    wide = 8 * HD
    by_rows = pl.BlockSpec((wide, ROWS), lambda i: (i, 0))
    by_columns = pl.BlockSpec((ROWS, wide), lambda i: (0, i))
    taps_columns = pl.BlockSpec((TAPS, wide), lambda i: (0, i))
    return pl.pallas_call(
        finish,
        grid=(WIDTH // wide,),
        out_shape=(local, local, local, local, taps_out),
        in_specs=[by_rows] * 3 + [by_columns, taps_columns],
        out_specs=[by_columns] * 4 + [taps_columns],
    )(dq, dk, dv, gb, gk)


def solution(mesh):
    split = P(("ctx", "seq"), None)
    return jax.shard_map(
        on_device,
        mesh=mesh,
        in_specs=(split, split, split, split, split, P(), split, P("ctx")),
        out_specs=(split, split, split, split, P()),
        check_vma=False,
    )
```

```python
import functools
import math

import jax
import jax.numpy as jnp
from jax import lax
from jax.experimental import pallas as pl
from jax.experimental.pallas import tpu as pltpu
from jax.sharding import PartitionSpec as P

BF = jnp.bfloat16
F32 = jnp.float32
HD = 96
HEADS = 16
ROWS = 128
WIDTH = HEADS * HD
SEG = 2048
TAPS = 32
LANES = 128
GROUPS = WIDTH // LANES
QB = 256
NB = SEG // QB
NZ = 16
RIM = 16
STEPS = ((1, 2), (1, 1), (1, 3), (0, 2), (1, 0), (0, 1), (0, 3), (0, 0))
BACK = tuple(STEPS.index((-y % 2, -x % 4)) for y, x in STEPS)
OWN = 2 * (len(STEPS) - 1)
SCALE = 1.0 / math.sqrt(HD)
EXP2_SCALE = SCALE * math.log2(math.e)
MESH = pl.DeviceIdType.MESH


def dot(a, b):
    return lax.dot_general(a, b, (((1,), (0,)), ((), ())), preferred_element_type=F32)


def block(index, size):
    if isinstance(index, int):
        return pl.ds(index * size, size)
    return pl.ds(pl.multiple_of(index * size, size), size)


def halves(x):
    return [x[:, c * LANES : (c + 1) * LANES] for c in range(x.shape[1] // LANES)]


def kernel(
    q_hbm, k_hbm, v_hbm, x_hbm, go_hbm, taps_hbm, bits_hbm, len_ref,
    dq_in, dk_in, dv_in, gb_hbm, gk_ref,
    q_ref, k_ref, v_ref, x_ref, go_ref, taps_ref, bits_ref, gb_ref,
    x_pad, g_pad, go_wide, gi_wide, x_rim, go_rim, keep_t,
    part, pair_in, half, z_in, x_out, x_in, y_out, y_in, full_out, full_z, full_pair,
    q_loc, k_loc, v_loc, a_loc, q_t, k_t, v_t, a_t,
    q_n, k_n, a_n, k_aug, v_aug, prob, dscore, work, inv_ref, side, q_side,
    dq_t, dk_t, dv_t,
    in_send, in_recv, out_send, out_recv, rim_send, rim_recv, sum_send, sum_recv, load_sem, own_sem,
):
    seq = lax.axis_index("seq")
    ctx = lax.axis_index("ctx")
    chip = seq // 2
    core = seq % 2
    sibling = chip * 2 + (1 - core)
    y_hi = ctx // NZ
    z = ctx % NZ
    at_x = chip % 4
    at_y = y_hi * 2 + chip // 4
    place = ctx * 16 + seq
    total = 512
    before = lax.rem(place + total - 1, total)
    after = lax.rem(place + 1, total)
    before_id = (before % 16, before // 16)
    after_id = (after % 16, after // 16)
    length = len_ref[0]

    def remote(src, dst, send, recv, device):
        return pltpu.make_async_remote_copy(
            src_ref=src, dst_ref=dst, send_sem=send, recv_sem=recv,
            device_id=device, device_id_type=MESH,
        )

    loads = [
        pltpu.make_async_copy(src, dst, load_sem.at[n])
        for n, (src, dst) in enumerate(
            (
                (q_hbm, q_ref), (x_hbm, x_ref), (go_hbm, go_ref),
                (k_hbm, k_ref), (v_hbm, v_ref), (taps_hbm, taps_ref),
                (bits_hbm, bits_ref),
            )
        )
    ]
    for load in loads:
        load.start()
    q_load, x_load, go_load, k_load, v_load, taps_load, bits_load = loads

    barrier = pltpu.get_barrier_semaphore()

    def greet(device):
        pl.semaphore_signal(barrier, inc=1, device_id=device, device_id_type=MESH)

    greet(before_id)
    greet(after_id)

    def greet_some(r, carry):
        greet((lax.rem(seq + r, 16), ctx))
        greet((seq, y_hi * NZ + lax.rem(z + r, NZ)))
        return carry

    lax.fori_loop(1, 16, greet_some, 0)

    for low in range(2):
        greet(((low * 4 + at_x) * 2 + core, (1 - y_hi) * NZ + z))

    def turn(src, dst):
        for j in range(GROUPS):
            s = slice(j * LANES, (j + 1) * LANES)
            dst[s, :] = src[:, s].T

    def tile_at(i):
        y, x = STEPS[i]
        return lax.rem(chip // 4 + y, 2) * 4 + lax.rem(chip % 4 + x, 4)

    def peers_at(i):
        tile = tile_at(i)
        return (tile * 2, tile * 2 + 1) if i < NB - 1 else (sibling,)

    def send_in(n, loc, got):
        for i in range(NB):
            for peer in peers_at(i):
                remote(
                    loc.at[block(peer, HD), :], got.at[:, block(2 * BACK[i] + core, ROWS)],
                    in_send.at[n], in_recv.at[n], (peer, ctx),
                ).start()
        got[:, block(OWN + core, ROWS)] = loc[block(seq, HD), :]

    def wait_in(n, loc, got):
        remote(
            loc.at[: 15 * HD, :], got.at[:, : 15 * ROWS],
            in_send.at[n], in_recv.at[n], (sibling, ctx),
        ).wait_recv()

    q_load.wait()
    turn(q_ref, q_loc)
    x_load.wait()
    go_load.wait()
    pl.semaphore_wait(barrier, 2 + 15 + 15 + 2)

    rims = []
    for n, (src, got, size) in enumerate(((x_ref, x_rim, 2 * RIM), (go_ref, go_rim, RIM))):
        rims.append(
            remote(
                src.at[:size, :], got.at[1], rim_send.at[n, 0], rim_recv.at[n, 0], before_id
            )
        )
        rims.append(
            remote(
                src.at[ROWS - size :, :], got.at[0],
                rim_send.at[n, 1], rim_recv.at[n, 1], after_id,
            )
        )
    for rim in rims:
        rim.start()
    send_in(0, q_loc, q_t)
    k_load.wait()
    turn(k_ref, k_loc)
    send_in(1, k_loc, k_t)
    v_load.wait()
    turn(v_ref, v_loc)
    send_in(2, v_loc, v_t)

    def widen(dst, start, src, factor=None):
        for c in range(GROUPS):
            piece = src[:, c * LANES : (c + 1) * LANES].astype(F32)
            dst[c, start : start + piece.shape[0], :] = piece if factor is None else piece * factor

    widen(x_pad, 2 * RIM, x_ref)
    widen(go_wide, RIM, go_ref)
    has_before = (place > 0).astype(F32)
    has_after = (place < total - 1).astype(F32)
    taps_load.wait()
    bits_load.wait()
    for rim in rims:
        rim.wait_recv()
    widen(x_pad, 0, x_rim.at[0], has_before)
    widen(x_pad, 2 * RIM + ROWS, x_rim.at[1], has_after)
    widen(go_wide, 0, go_rim.at[0], has_before)
    widen(go_wide, RIM + ROWS, go_rim.at[1], has_after)

    def rows(ref, p, c, stride=16):
        return ref[c, pl.ds(p, 8, stride=stride), :]

    def forward(c, carry):
        cs = block(c, LANES)
        acc = [jnp.zeros((8, LANES), F32) for _ in range(20)]
        xs = [rows(x_pad, p, c, 20) for p in range(1, 52)]
        for j in range(TAPS):
            tap = jnp.broadcast_to(taps_ref[j : j + 1, cs], (8, LANES))
            for i in range(20):
                acc[i] = acc[i] + tap * xs[i + j]
        for i in range(20):
            pre = acc[i]
            sig = jax.nn.sigmoid(pre)
            slope = sig * (1.0 + pre * (1.0 - sig))
            grad = (rows(go_wide, i, c, 20) * slope).astype(BF).astype(F32)
            g_pad[c, pl.ds(i, 8, stride=20), :] = grad
        return carry

    lax.fori_loop(0, GROUPS, forward, 0)

    def backward(c, carry):
        cs = block(c, LANES)
        gs = [rows(g_pad, p, c) for p in range(47)]
        acc = [rows(go_wide, RIM + i, c) for i in range(16)]
        for j in range(TAPS):
            tap = jnp.broadcast_to(taps_ref[j : j + 1, cs], (8, LANES))
            for i in range(16):
                acc[i] = acc[i] + tap * gs[i + 31 - j]
        for i in range(16):
            gi_wide[c, pl.ds(i, 8, stride=16), :] = acc[i]
        return carry

    lax.fori_loop(0, GROUPS, backward, 0)

    row_bit = lax.broadcasted_iota(jnp.int32, (32, HEADS), 0)
    planes = [
        lax.shift_right_logical(jnp.broadcast_to(bits_ref[w : w + 1, :], (32, HEADS)), row_bit) & 1
        for w in range(ROWS // 32)
    ]
    keep = (1 - jnp.concatenate(planes, axis=0)).astype(F32) * (4.0 / 3.0)
    keep = jnp.concatenate([keep, jnp.zeros((ROWS, LANES - HEADS), F32)], axis=1).T[:HEADS]
    frame = seq * ROWS + lax.broadcasted_iota(jnp.int32, (HEADS, ROWS), 1)
    keep_t[...] = keep * jnp.where(frame < length, 1.0, 0.0)

    for j in range(GROUPS):
        s = slice(j * LANES, (j + 1) * LANES)
        wide = gi_wide[j]
        gb_ref[:, s] = wide.astype(BF)
        turned = wide.T
        for at in range(0, LANES, 32):
            head = (j * LANES + at) // HD
            piece = turned[at : at + 32] * keep_t[head : head + 1, :]
            a_loc[j * LANES + at : j * LANES + at + 32, :] = piece.astype(BF)
    send_in(3, a_loc, a_t)
    gb_store = pltpu.make_async_copy(gb_ref, gb_hbm, own_sem.at[3])
    gb_store.start()

    def tap_grads(c, carry):
        cs = block(c, LANES)
        xs = [rows(x_pad, p, c) for p in range(17, 64)]
        acc = [jnp.zeros((8, LANES), F32) for _ in range(TAPS)]
        for i in range(16):
            grad = rows(g_pad, RIM + i, c)
            for j in range(TAPS):
                acc[j] = acc[j] + grad * xs[i + j]
        for j in range(TAPS):
            part[j : j + 1, cs] = jnp.sum(acc[j], axis=0, keepdims=True)
        return carry

    lax.fori_loop(0, GROUPS, tap_grads, 0)
    sum_a = remote(
        part.at[block(1 - core, 16), :], pair_in, sum_send.at[0], sum_recv.at[0], (sibling, ctx)
    )
    sum_a.start()

    sum_a.wait_recv()
    mine = part[block(core, 16), :] + pair_in[...]
    for t in range(16):
        half[t] = mine[t : t + 1, :]

    def send_z(src, dst, n, whole):
        def one(r, carry):
            other = lax.rem(z + r, NZ)
            remote(
                src if whole else src.at[other], dst.at[z],
                sum_send.at[n], sum_recv.at[n], (seq, y_hi * NZ + other),
            ).start()
            return carry

        lax.fori_loop(1, NZ, one, 0)

    def wait_sum(n, buf):
        others = buf.at[: buf.shape[0] - 1]
        remote(others, others, sum_send.at[n], sum_recv.at[n], (sibling, ctx)).wait_recv()

    send_z(half, z_in, 1, False)
    z_in[z] = half[z]

    tail_row = lax.broadcasted_iota(jnp.int32, (LANES - HD, LANES), 0)
    ones_row = jnp.where(tail_row == 0, 1.0, 0.0).astype(BF)
    zero_rows = jnp.zeros((LANES - HD, LANES), BF)

    def natural(dst, src, tail):
        for j in range(SEG // LANES):
            s = slice(j * LANES, (j + 1) * LANES)
            dst[s, :] = jnp.concatenate([src[:, s], tail], axis=0).T

    wait_in(0, q_loc, q_t)
    natural(q_n, q_t, ones_row)
    wait_in(1, k_loc, k_t)
    natural(k_n, k_t, zero_rows)
    k_aug[:HD, :] = k_t[...]
    bias_row = lax.broadcasted_iota(jnp.int32, (LANES - HD, QB), 0)
    lane = lax.broadcasted_iota(jnp.int32, (LANES - HD, QB), 1)
    for i in range(NB):
        dead = (bias_row == 0) & (tile_at(i) * QB + lane >= length)
        k_aug[HD:, i * QB : (i + 1) * QB] = jnp.where(dead, -1e30, 0.0).astype(BF)
    v_aug[HD:, :] = jnp.zeros((LANES - HD, SEG), BF)

    def scores(i):
        queries = q_n[i * QB : (i + 1) * QB, :]
        top = None
        for k in range(NB):
            ks = slice(k * QB, (k + 1) * QB)
            s = dot(queries, k_aug[:, ks])
            work[i % 2, :, ks] = s
            for t in halves(s):
                top = t if top is None else jnp.maximum(top, t)
        return jnp.max(top, axis=1, keepdims=True)

    def softmax(i, top):
        r = slice(i * QB, (i + 1) * QB)
        count = None
        for k in range(NB):
            ks = slice(k * QB, (k + 1) * QB)
            p = jnp.exp2((work[i % 2, :, ks] - top) * EXP2_SCALE).astype(BF)
            prob[r, ks] = p
            for t in halves(p.astype(F32)):
                count = t if count is None else count + t
        inv_ref[r, :] = 1.0 / jnp.sum(count, axis=1, keepdims=True)

    top = scores(0)
    for i in range(NB):
        next_top = scores(i + 1) if i + 1 < NB else None
        softmax(i, top)
        top = next_top

    for j in range(SEG // LANES):
        s = slice(j * LANES, (j + 1) * LANES)
        q_side[:, s] = (q_n[s, :].astype(F32) * (inv_ref[s, :] * SCALE)).astype(BF).T[:HD]

    def add_up(buf):
        value = buf[0]
        for t in range(1, buf.shape[0]):
            value = value + buf[t]
        return value

    wait_sum(1, z_in)
    x_out[...] = add_up(z_in)
    x_in[at_x] = x_out[...]
    for r in range(1, 4):
        other = (chip // 4) * 4 + lax.rem(at_x + r, 4)
        remote(
            x_out, x_in.at[at_x], sum_send.at[2], sum_recv.at[2], (other * 2 + core, ctx)
        ).start()

    def send_out(n, src, dst, i):
        for c, peer in enumerate(peers_at(i)):
            at = 2 * i + c if i < NB - 1 else OWN + 1 - core
            remote(
                src.at[:, block(at, ROWS)], dst.at[block(seq, HD), :],
                out_send.at[n], out_recv.at[n], (peer, ctx),
            ).start()

    def keep_own(n, src, dst):
        copy = pltpu.make_async_copy(
            src.at[:, block(OWN + core, ROWS)], dst.at[block(seq, HD), :], own_sem.at[n]
        )
        copy.start()
        return copy

    def wait_out(n, src, dst):
        remote(
            src.at[:, : 15 * ROWS], dst.at[: 15 * HD, :],
            out_send.at[n], out_recv.at[n], (sibling, ctx),
        ).wait_recv()

    def columns(n, left, right, src, dst):
        for i in range(NB):
            s = slice(i * QB, (i + 1) * QB)
            src[:, s] = dot(left[...], right[:, s]).astype(BF)
            send_out(n, src, dst, i)
        return keep_own(n, src, dst)

    wait_in(2, v_loc, v_t)
    v_aug[:HD, :] = v_t[...]
    wait_in(3, a_loc, a_t)
    natural(a_n, a_t, zero_rows)
    for j in range(SEG // LANES):
        s = slice(j * LANES, (j + 1) * LANES)
        side[:, s] = (a_n[s, :].astype(F32) * inv_ref[s, :]).astype(BF).T[:HD]
    wait_sum(2, x_in)
    y_out[...] = add_up(x_in)
    y_in[at_y] = y_out[...]
    for r in range(1, 4):
        other = lax.rem(at_y + r, 4)
        remote(
            y_out, y_in.at[at_y], sum_send.at[5], sum_recv.at[5],
            (((other % 2) * 4 + at_x) * 2 + core, (other // 2) * NZ + z),
        ).start()

    dv_own = columns(2, side, prob, dv_t, dv_in)

    def grad_probs(i):
        r = slice(i * QB, (i + 1) * QB)
        grads = a_n[r, :]
        acc = None
        for k in range(NB):
            ks = slice(k * QB, (k + 1) * QB)
            g = dot(grads, v_aug[:, ks])
            work[i % 2, :, ks] = g
            for t in halves(g * prob[r, ks].astype(F32)):
                acc = t if acc is None else acc + t
        return acc

    def grad_scores(i, acc):
        r = slice(i * QB, (i + 1) * QB)
        inverse = inv_ref[r, :]
        delta = jnp.sum(acc, axis=1, keepdims=True) * inverse
        for k in range(NB):
            ks = slice(k * QB, (k + 1) * QB)
            ds = prob[r, ks].astype(F32) * (work[i % 2, :, ks] - delta)
            dscore[r, ks] = ds.astype(BF)
        dq = (dot(dscore[r, :], k_n[...]) * (inverse * SCALE)).astype(BF)
        for j in range(QB // LANES):
            dq_t[:, i * QB + j * LANES : i * QB + (j + 1) * LANES] = dq[j * LANES : (j + 1) * LANES, :].T[:HD]
        send_out(0, dq_t, dq_in, i)

    acc = grad_probs(0)
    for i in range(NB):
        next_acc = grad_probs(i + 1) if i + 1 < NB else None
        grad_scores(i, acc)
        acc = next_acc
    dq_own = keep_own(0, dq_t, dq_in)

    wait_sum(5, y_in)
    full_out[...] = add_up(y_in) * (1.0 / 32.0)
    full_z[z] = full_out[...]
    send_z(full_out, full_z, 3, True)

    dk_own = columns(1, q_side, dscore, dk_t, dk_in)

    wait_sum(3, full_z)
    sum_e = remote(full_z, full_pair, sum_send.at[4], sum_recv.at[4], (sibling, ctx))
    sum_e.start()
    sum_e.wait_recv()
    first = core == 0
    for t in range(16):
        own, got = full_z[t], full_pair[t]
        gk_ref[t : t + 1, :] = jnp.where(first, own, got)
        gk_ref[16 + t : 17 + t, :] = jnp.where(first, got, own)

    for n, (src, dst) in enumerate(((dq_t, dq_in), (dk_t, dk_in), (dv_t, dv_in))):
        wait_out(n, src, dst)
    for copy in (dq_own, dk_own, dv_own, gb_store):
        copy.wait()

    for n, (loc, got) in enumerate(((q_loc, q_t), (k_loc, k_t), (v_loc, v_t), (a_loc, a_t))):
        remote(
            loc.at[: 15 * HD, :], got.at[:, : 15 * ROWS],
            in_send.at[n], in_recv.at[n], (sibling, ctx),
        ).wait_send()
    for n, (src, dst) in enumerate(((dq_t, dq_in), (dk_t, dk_in), (dv_t, dv_in))):
        remote(
            src.at[:, : 15 * ROWS], dst.at[: 15 * HD, :],
            out_send.at[n], out_recv.at[n], (sibling, ctx),
        ).wait_send()
    for copy in (*rims, sum_a, sum_e):
        copy.wait_send()
    for n, buf in ((1, z_in), (2, x_in), (5, y_in), (3, full_z)):
        others = buf.at[: buf.shape[0] - 1]
        remote(others, others, sum_send.at[n], sum_recv.at[n], (sibling, ctx)).wait_send()


def on_device(
    queries, key_rows, value_rows, block_in, grad_out, conv_kernel, drop_bits, seg_length
):
    vmem = pl.BlockSpec(memory_space=pltpu.VMEM)
    smem = pl.BlockSpec(memory_space=pltpu.SMEM)
    local = jax.ShapeDtypeStruct((ROWS, WIDTH), BF)
    dma = pltpu.SemaphoreType.DMA
    scratch = [
        *[pltpu.VMEM((ROWS, WIDTH), BF) for _ in range(5)],
        pltpu.VMEM((TAPS, WIDTH), F32),
        pltpu.VMEM((ROWS // 32, HEADS), jnp.int32),
        pltpu.VMEM((ROWS, WIDTH), BF),
        pltpu.VMEM((GROUPS, ROWS + 4 * RIM, LANES), F32),
        pltpu.VMEM((GROUPS, ROWS + 2 * RIM, LANES), F32),
        pltpu.VMEM((GROUPS, ROWS + 2 * RIM, LANES), F32),
        pltpu.VMEM((GROUPS, ROWS, LANES), F32),
        pltpu.VMEM((2, 2 * RIM, WIDTH), BF),
        pltpu.VMEM((2, RIM, WIDTH), BF),
        pltpu.VMEM((HEADS, ROWS), F32),
        pltpu.VMEM((TAPS, WIDTH), F32),
        pltpu.VMEM((16, WIDTH), F32),
        pltpu.VMEM((16, 1, WIDTH), F32),
        pltpu.VMEM((16, 1, WIDTH), F32),
        pltpu.VMEM((1, WIDTH), F32),
        pltpu.VMEM((4, 1, WIDTH), F32),
        pltpu.VMEM((1, WIDTH), F32),
        pltpu.VMEM((4, 1, WIDTH), F32),
        pltpu.VMEM((1, WIDTH), F32),
        pltpu.VMEM((16, 1, WIDTH), F32),
        pltpu.VMEM((16, 1, WIDTH), F32),
        *[pltpu.VMEM((WIDTH, ROWS), BF) for _ in range(4)],
        *[pltpu.VMEM((HD, SEG), BF) for _ in range(4)],
        *[pltpu.VMEM((SEG, LANES), BF) for _ in range(3)],
        *[pltpu.VMEM((LANES, SEG), BF) for _ in range(2)],
        pltpu.VMEM((SEG, SEG), BF),
        pltpu.VMEM((SEG, SEG), BF),
        pltpu.VMEM((2, QB, SEG), F32),
        pltpu.VMEM((SEG, 1), F32),
        pltpu.VMEM((HD, SEG), BF),
        pltpu.VMEM((HD, SEG), BF),
        *[pltpu.VMEM((HD, SEG), BF) for _ in range(3)],
        dma((4,)),
        dma((4,)),
        dma((3,)),
        dma((3,)),
        dma((2, 2)),
        dma((2, 2)),
        dma((6,)),
        dma((6,)),
        dma((7,)),
        dma((4,)),
    ]
    hbm = pl.BlockSpec(memory_space=pl.ANY)
    turned = jax.ShapeDtypeStruct((WIDTH, ROWS), BF)
    taps_out = jax.ShapeDtypeStruct((TAPS, WIDTH), F32)
    dq, dk, dv, gb, gk = pl.pallas_call(
        kernel,
        out_shape=(turned, turned, turned, local, taps_out),
        in_specs=[hbm] * 7 + [smem],
        out_specs=(hbm,) * 4 + (vmem,),
        scratch_shapes=scratch,
        compiler_params=pltpu.CompilerParams(
            collective_id=0, has_side_effects=True, vmem_limit_bytes=56 * 1024 * 1024
        ),
        cost_estimate=pl.CostEstimate(
            flops=5 * 2 * SEG * SEG * HD, bytes_accessed=4 << 20, transcendentals=SEG * SEG
        ),
    )(queries, key_rows, value_rows, block_in, grad_out, conv_kernel, drop_bits, seg_length)

    def finish(dq_i, dk_i, dv_i, gb_i, gk_i, dq_o, dk_o, dv_o, gb_o, gk_o):
        for src, dst in ((dq_i, dq_o), (dk_i, dk_o), (dv_i, dv_o)):
            for j in range(dst.shape[1] // LANES):
                s = slice(j * LANES, (j + 1) * LANES)
                dst[:, s] = src[s, :].T
        gb_o[...] = gb_i[...]
        gk_o[...] = gk_i[...]

    wide = 8 * HD
    by_rows = pl.BlockSpec((wide, ROWS), lambda i: (i, 0))
    by_columns = pl.BlockSpec((ROWS, wide), lambda i: (0, i))
    taps_columns = pl.BlockSpec((TAPS, wide), lambda i: (0, i))
    return pl.pallas_call(
        finish,
        grid=(WIDTH // wide,),
        out_shape=(local, local, local, local, taps_out),
        in_specs=[by_rows] * 3 + [by_columns, taps_columns],
        out_specs=[by_columns] * 4 + [taps_columns],
    )(dq, dk, dv, gb, gk)


def solution(mesh):
    split = P(("ctx", "seq"), None)
    return jax.shard_map(
        on_device,
        mesh=mesh,
        in_specs=(split, split, split, split, split, P(), split, P("ctx")),
        out_specs=(split, split, split, split, P()),
        check_vma=False,
    )
```

```python
import functools
import math

import jax
import jax.numpy as jnp
from jax import lax
from jax.experimental import pallas as pl
from jax.experimental.pallas import tpu as pltpu
from jax.sharding import PartitionSpec as P

BF = jnp.bfloat16
F32 = jnp.float32
HD = 96
HEADS = 16
ROWS = 128
WIDTH = HEADS * HD
SEG = 2048
TAPS = 32
LANES = 128
GROUPS = WIDTH // LANES
QB = 256
NB = SEG // QB
NZ = 16
RIM = 16
STEPS = ((1, 2), (1, 1), (1, 3), (0, 2), (1, 0), (0, 1), (0, 3), (0, 0))
BACK = tuple(STEPS.index((-y % 2, -x % 4)) for y, x in STEPS)
OWN = 2 * (len(STEPS) - 1)
SCALE = 1.0 / math.sqrt(HD)
EXP2_SCALE = SCALE * math.log2(math.e)
MESH = pl.DeviceIdType.MESH


def dot(a, b):
    return lax.dot_general(a, b, (((1,), (0,)), ((), ())), preferred_element_type=F32)


def block(index, size):
    if isinstance(index, int):
        return pl.ds(index * size, size)
    return pl.ds(pl.multiple_of(index * size, size), size)


def halves(x):
    return [x[:, c * LANES : (c + 1) * LANES] for c in range(x.shape[1] // LANES)]


def kernel(
    q_hbm, k_hbm, v_hbm, x_hbm, go_hbm, taps_hbm, bits_hbm, len_ref,
    dq_in, dk_in, dv_in, gb_hbm, gk_ref,
    q_ref, k_ref, v_ref, x_ref, go_ref, taps_ref, bits_ref, gb_ref,
    x_pad, g_pad, go_wide, gi_wide, x_rim, go_rim, keep_t,
    part, pair_in, half, z_in, x_out, x_in, y_out, y_in, full_out, full_z, full_pair,
    q_loc, k_loc, v_loc, a_loc, q_t, k_t, v_t, a_t,
    q_n, k_n, a_n, k_aug, v_aug, prob, dscore, work, inv_ref, side, q_side,
    dq_t, dk_t, dv_t,
    in_send, in_recv, out_send, out_recv, rim_send, rim_recv, sum_send, sum_recv, load_sem, own_sem,
):
    seq = lax.axis_index("seq")
    ctx = lax.axis_index("ctx")
    chip = seq // 2
    core = seq % 2
    sibling = chip * 2 + (1 - core)
    y_hi = ctx // NZ
    z = ctx % NZ
    at_x = chip % 4
    at_y = y_hi * 2 + chip // 4
    place = ctx * 16 + seq
    total = 512
    before = lax.rem(place + total - 1, total)
    after = lax.rem(place + 1, total)
    before_id = (before % 16, before // 16)
    after_id = (after % 16, after // 16)
    length = len_ref[0]

    def remote(src, dst, send, recv, device):
        return pltpu.make_async_remote_copy(
            src_ref=src, dst_ref=dst, send_sem=send, recv_sem=recv,
            device_id=device, device_id_type=MESH,
        )

    loads = [
        pltpu.make_async_copy(src, dst, load_sem.at[n])
        for n, (src, dst) in enumerate(
            (
                (q_hbm, q_ref), (x_hbm, x_ref), (go_hbm, go_ref),
                (k_hbm, k_ref), (v_hbm, v_ref), (taps_hbm, taps_ref),
                (bits_hbm, bits_ref),
            )
        )
    ]
    for load in loads:
        load.start()
    q_load, x_load, go_load, k_load, v_load, taps_load, bits_load = loads

    barrier = pltpu.get_barrier_semaphore()

    def greet(device):
        pl.semaphore_signal(barrier, inc=1, device_id=device, device_id_type=MESH)

    greet(before_id)
    greet(after_id)

    def greet_some(r, carry):
        greet((lax.rem(seq + r, 16), ctx))
        greet((seq, y_hi * NZ + lax.rem(z + r, NZ)))
        return carry

    lax.fori_loop(1, 16, greet_some, 0)

    for low in range(2):
        greet(((low * 4 + at_x) * 2 + core, (1 - y_hi) * NZ + z))

    def turn(src, dst):
        for j in range(GROUPS):
            s = slice(j * LANES, (j + 1) * LANES)
            dst[s, :] = src[:, s].T

    def tile_at(i):
        y, x = STEPS[i]
        return lax.rem(chip // 4 + y, 2) * 4 + lax.rem(chip % 4 + x, 4)

    def peers_at(i):
        tile = tile_at(i)
        return (tile * 2, tile * 2 + 1) if i < NB - 1 else (sibling,)

    def send_in(n, loc, got):
        for i in range(NB):
            for peer in peers_at(i):
                remote(
                    loc.at[block(peer, HD), :], got.at[:, block(2 * BACK[i] + core, ROWS)],
                    in_send.at[n], in_recv.at[n], (peer, ctx),
                ).start()
        got[:, block(OWN + core, ROWS)] = loc[block(seq, HD), :]

    def wait_in(n, loc, got):
        remote(
            loc.at[: 15 * HD, :], got.at[:, : 15 * ROWS],
            in_send.at[n], in_recv.at[n], (sibling, ctx),
        ).wait_recv()

    q_load.wait()
    turn(q_ref, q_loc)
    x_load.wait()
    go_load.wait()
    pl.semaphore_wait(barrier, 2 + 15 + 15 + 2)

    rims = []
    for n, (src, got, size) in enumerate(((x_ref, x_rim, 2 * RIM), (go_ref, go_rim, RIM))):
        rims.append(
            remote(
                src.at[:size, :], got.at[1], rim_send.at[n, 0], rim_recv.at[n, 0], before_id
            )
        )
        rims.append(
            remote(
                src.at[ROWS - size :, :], got.at[0],
                rim_send.at[n, 1], rim_recv.at[n, 1], after_id,
            )
        )
    for rim in rims:
        rim.start()
    send_in(0, q_loc, q_t)
    k_load.wait()
    turn(k_ref, k_loc)
    send_in(1, k_loc, k_t)
    v_load.wait()
    turn(v_ref, v_loc)
    send_in(2, v_loc, v_t)

    def widen(dst, start, src, factor=None):
        for c in range(GROUPS):
            piece = src[:, c * LANES : (c + 1) * LANES].astype(F32)
            dst[c, start : start + piece.shape[0], :] = piece if factor is None else piece * factor

    widen(x_pad, 2 * RIM, x_ref)
    widen(go_wide, RIM, go_ref)
    has_before = (place > 0).astype(F32)
    has_after = (place < total - 1).astype(F32)
    taps_load.wait()
    bits_load.wait()
    for rim in rims:
        rim.wait_recv()
    widen(x_pad, 0, x_rim.at[0], has_before)
    widen(x_pad, 2 * RIM + ROWS, x_rim.at[1], has_after)
    widen(go_wide, 0, go_rim.at[0], has_before)
    widen(go_wide, RIM + ROWS, go_rim.at[1], has_after)

    def rows(ref, p, c, stride=16):
        return ref[c, pl.ds(p, 8, stride=stride), :]

    def forward(c, carry):
        cs = block(c, LANES)
        acc = [jnp.zeros((8, LANES), F32) for _ in range(20)]
        xs = [rows(x_pad, p, c, 20) for p in range(1, 52)]
        for j in range(TAPS):
            tap = jnp.broadcast_to(taps_ref[j : j + 1, cs], (8, LANES))
            for i in range(20):
                acc[i] = acc[i] + tap * xs[i + j]
        for i in range(20):
            pre = acc[i]
            sig = jax.nn.sigmoid(pre)
            slope = sig * (1.0 + pre * (1.0 - sig))
            grad = (rows(go_wide, i, c, 20) * slope).astype(BF).astype(F32)
            g_pad[c, pl.ds(i, 8, stride=20), :] = grad
        return carry

    lax.fori_loop(0, GROUPS, forward, 0)

    def backward(c, carry):
        cs = block(c, LANES)
        gs = [rows(g_pad, p, c) for p in range(47)]
        acc = [rows(go_wide, RIM + i, c) for i in range(16)]
        for j in range(TAPS):
            tap = jnp.broadcast_to(taps_ref[j : j + 1, cs], (8, LANES))
            for i in range(16):
                acc[i] = acc[i] + tap * gs[i + 31 - j]
        for i in range(16):
            gi_wide[c, pl.ds(i, 8, stride=16), :] = acc[i]
        return carry

    lax.fori_loop(0, GROUPS, backward, 0)

    row_bit = lax.broadcasted_iota(jnp.int32, (32, HEADS), 0)
    planes = [
        lax.shift_right_logical(jnp.broadcast_to(bits_ref[w : w + 1, :], (32, HEADS)), row_bit) & 1
        for w in range(ROWS // 32)
    ]
    keep = (1 - jnp.concatenate(planes, axis=0)).astype(F32) * (4.0 / 3.0)
    keep = jnp.concatenate([keep, jnp.zeros((ROWS, LANES - HEADS), F32)], axis=1).T[:HEADS]
    frame = seq * ROWS + lax.broadcasted_iota(jnp.int32, (HEADS, ROWS), 1)
    keep_t[...] = keep * jnp.where(frame < length, 1.0, 0.0)

    for j in range(GROUPS):
        s = slice(j * LANES, (j + 1) * LANES)
        wide = gi_wide[j]
        gb_ref[:, s] = wide.astype(BF)
        turned = wide.T
        for at in range(0, LANES, 32):
            head = (j * LANES + at) // HD
            piece = turned[at : at + 32] * keep_t[head : head + 1, :]
            a_loc[j * LANES + at : j * LANES + at + 32, :] = piece.astype(BF)
    send_in(3, a_loc, a_t)
    gb_store = pltpu.make_async_copy(gb_ref, gb_hbm, own_sem.at[3])
    gb_store.start()

    def tap_grads(c, carry):
        cs = block(c, LANES)
        xs = [rows(x_pad, p, c) for p in range(17, 64)]
        acc = [jnp.zeros((8, LANES), F32) for _ in range(TAPS)]
        for i in range(16):
            grad = rows(g_pad, RIM + i, c)
            for j in range(TAPS):
                acc[j] = acc[j] + grad * xs[i + j]
        for j in range(TAPS):
            part[j : j + 1, cs] = jnp.sum(acc[j], axis=0, keepdims=True)
        return carry

    lax.fori_loop(0, GROUPS, tap_grads, 0)
    sum_a = remote(
        part.at[block(1 - core, 16), :], pair_in, sum_send.at[0], sum_recv.at[0], (sibling, ctx)
    )
    sum_a.start()

    sum_a.wait_recv()
    mine = part[block(core, 16), :] + pair_in[...]
    for t in range(16):
        half[t] = mine[t : t + 1, :]

    def send_z(src, dst, n, whole):
        def one(r, carry):
            other = lax.rem(z + r, NZ)
            remote(
                src if whole else src.at[other], dst.at[z],
                sum_send.at[n], sum_recv.at[n], (seq, y_hi * NZ + other),
            ).start()
            return carry

        lax.fori_loop(1, NZ, one, 0)

    def wait_sum(n, buf):
        others = buf.at[: buf.shape[0] - 1]
        remote(others, others, sum_send.at[n], sum_recv.at[n], (sibling, ctx)).wait_recv()

    send_z(half, z_in, 1, False)
    z_in[z] = half[z]

    tail_row = lax.broadcasted_iota(jnp.int32, (LANES - HD, LANES), 0)
    ones_row = jnp.where(tail_row == 0, 1.0, 0.0).astype(BF)
    zero_rows = jnp.zeros((LANES - HD, LANES), BF)

    def natural(dst, src, tail):
        for j in range(SEG // LANES):
            s = slice(j * LANES, (j + 1) * LANES)
            dst[s, :] = jnp.concatenate([src[:, s], tail], axis=0).T

    wait_in(0, q_loc, q_t)
    natural(q_n, q_t, ones_row)
    wait_in(1, k_loc, k_t)
    natural(k_n, k_t, zero_rows)
    k_aug[:HD, :] = k_t[...]
    bias_row = lax.broadcasted_iota(jnp.int32, (LANES - HD, QB), 0)
    lane = lax.broadcasted_iota(jnp.int32, (LANES - HD, QB), 1)
    for i in range(NB):
        dead = (bias_row == 0) & (tile_at(i) * QB + lane >= length)
        k_aug[HD:, i * QB : (i + 1) * QB] = jnp.where(dead, -1e30, 0.0).astype(BF)
    v_aug[HD:, :] = jnp.zeros((LANES - HD, SEG), BF)

    def scores(i):
        queries = q_n[i * QB : (i + 1) * QB, :]
        top = None
        for k in range(NB):
            ks = slice(k * QB, (k + 1) * QB)
            s = dot(queries, k_aug[:, ks])
            work[i % 2, :, ks] = s
            for t in halves(s):
                top = t if top is None else jnp.maximum(top, t)
        return jnp.max(top, axis=1, keepdims=True)

    def softmax(i, top):
        r = slice(i * QB, (i + 1) * QB)
        count = None
        for k in range(NB):
            ks = slice(k * QB, (k + 1) * QB)
            p = jnp.exp2((work[i % 2, :, ks] - top) * EXP2_SCALE).astype(BF)
            prob[r, ks] = p
            for t in halves(p.astype(F32)):
                count = t if count is None else count + t
        inv_ref[r, :] = 1.0 / jnp.sum(count, axis=1, keepdims=True)

    top = scores(0)
    for i in range(NB):
        next_top = scores(i + 1) if i + 1 < NB else None
        softmax(i, top)
        top = next_top

    for j in range(SEG // LANES):
        s = slice(j * LANES, (j + 1) * LANES)
        q_side[:, s] = (q_n[s, :].astype(F32) * (inv_ref[s, :] * SCALE)).astype(BF).T[:HD]

    def add_up(buf):
        value = buf[0]
        for t in range(1, buf.shape[0]):
            value = value + buf[t]
        return value

    wait_sum(1, z_in)
    x_out[...] = add_up(z_in)
    x_in[at_x] = x_out[...]
    for r in range(1, 4):
        other = (chip // 4) * 4 + lax.rem(at_x + r, 4)
        remote(
            x_out, x_in.at[at_x], sum_send.at[2], sum_recv.at[2], (other * 2 + core, ctx)
        ).start()

    def send_out(n, src, dst, i):
        for c, peer in enumerate(peers_at(i)):
            at = 2 * i + c if i < NB - 1 else OWN + 1 - core
            remote(
                src.at[:, block(at, ROWS)], dst.at[block(seq, HD), :],
                out_send.at[n], out_recv.at[n], (peer, ctx),
            ).start()

    def keep_own(n, src, dst):
        copy = pltpu.make_async_copy(
            src.at[:, block(OWN + core, ROWS)], dst.at[block(seq, HD), :], own_sem.at[n]
        )
        copy.start()
        return copy

    def wait_out(n, src, dst):
        remote(
            src.at[:, : 15 * ROWS], dst.at[: 15 * HD, :],
            out_send.at[n], out_recv.at[n], (sibling, ctx),
        ).wait_recv()

    def columns(n, left, right, src, dst):
        for i in range(NB):
            s = slice(i * QB, (i + 1) * QB)
            src[:, s] = dot(left[...], right[:, s]).astype(BF)
            send_out(n, src, dst, i)
        return keep_own(n, src, dst)

    wait_in(2, v_loc, v_t)
    v_aug[:HD, :] = v_t[...]
    wait_in(3, a_loc, a_t)
    natural(a_n, a_t, zero_rows)
    for j in range(SEG // LANES):
        s = slice(j * LANES, (j + 1) * LANES)
        side[:, s] = (a_n[s, :].astype(F32) * inv_ref[s, :]).astype(BF).T[:HD]

    dv_own = columns(2, side, prob, dv_t, dv_in)

    wait_sum(2, x_in)
    y_out[...] = add_up(x_in)
    y_in[at_y] = y_out[...]
    for r in range(1, 4):
        other = lax.rem(at_y + r, 4)
        remote(
            y_out, y_in.at[at_y], sum_send.at[5], sum_recv.at[5],
            (((other % 2) * 4 + at_x) * 2 + core, (other // 2) * NZ + z),
        ).start()

    def grad_probs(i):
        r = slice(i * QB, (i + 1) * QB)
        grads = a_n[r, :]
        acc = None
        for k in range(NB):
            ks = slice(k * QB, (k + 1) * QB)
            g = dot(grads, v_aug[:, ks])
            work[i % 2, :, ks] = g
            for t in halves(g * prob[r, ks].astype(F32)):
                acc = t if acc is None else acc + t
        return acc

    def grad_scores(i, acc):
        r = slice(i * QB, (i + 1) * QB)
        inverse = inv_ref[r, :]
        delta = jnp.sum(acc, axis=1, keepdims=True) * inverse
        for k in range(NB):
            ks = slice(k * QB, (k + 1) * QB)
            ds = prob[r, ks].astype(F32) * (work[i % 2, :, ks] - delta)
            dscore[r, ks] = ds.astype(BF)
        dq = (dot(dscore[r, :], k_n[...]) * (inverse * SCALE)).astype(BF)
        for j in range(QB // LANES):
            dq_t[:, i * QB + j * LANES : i * QB + (j + 1) * LANES] = dq[j * LANES : (j + 1) * LANES, :].T[:HD]
        send_out(0, dq_t, dq_in, i)

    acc = grad_probs(0)
    for i in range(NB):
        next_acc = grad_probs(i + 1) if i + 1 < NB else None
        grad_scores(i, acc)
        acc = next_acc
    dq_own = keep_own(0, dq_t, dq_in)

    wait_sum(5, y_in)
    full_out[...] = add_up(y_in) * (1.0 / 32.0)
    full_z[z] = full_out[...]
    send_z(full_out, full_z, 3, True)

    dk_own = columns(1, q_side, dscore, dk_t, dk_in)

    wait_sum(3, full_z)
    sum_e = remote(full_z, full_pair, sum_send.at[4], sum_recv.at[4], (sibling, ctx))
    sum_e.start()
    sum_e.wait_recv()
    first = core == 0
    for t in range(16):
        own, got = full_z[t], full_pair[t]
        gk_ref[t : t + 1, :] = jnp.where(first, own, got)
        gk_ref[16 + t : 17 + t, :] = jnp.where(first, got, own)

    for n, (src, dst) in enumerate(((dq_t, dq_in), (dk_t, dk_in), (dv_t, dv_in))):
        wait_out(n, src, dst)
    for copy in (dq_own, dk_own, dv_own, gb_store):
        copy.wait()

    for n, (loc, got) in enumerate(((q_loc, q_t), (k_loc, k_t), (v_loc, v_t), (a_loc, a_t))):
        remote(
            loc.at[: 15 * HD, :], got.at[:, : 15 * ROWS],
            in_send.at[n], in_recv.at[n], (sibling, ctx),
        ).wait_send()
    for n, (src, dst) in enumerate(((dq_t, dq_in), (dk_t, dk_in), (dv_t, dv_in))):
        remote(
            src.at[:, : 15 * ROWS], dst.at[: 15 * HD, :],
            out_send.at[n], out_recv.at[n], (sibling, ctx),
        ).wait_send()
    for copy in (*rims, sum_a, sum_e):
        copy.wait_send()
    for n, buf in ((1, z_in), (2, x_in), (5, y_in), (3, full_z)):
        others = buf.at[: buf.shape[0] - 1]
        remote(others, others, sum_send.at[n], sum_recv.at[n], (sibling, ctx)).wait_send()


def on_device(
    queries, key_rows, value_rows, block_in, grad_out, conv_kernel, drop_bits, seg_length
):
    vmem = pl.BlockSpec(memory_space=pltpu.VMEM)
    smem = pl.BlockSpec(memory_space=pltpu.SMEM)
    local = jax.ShapeDtypeStruct((ROWS, WIDTH), BF)
    dma = pltpu.SemaphoreType.DMA
    scratch = [
        *[pltpu.VMEM((ROWS, WIDTH), BF) for _ in range(5)],
        pltpu.VMEM((TAPS, WIDTH), F32),
        pltpu.VMEM((ROWS // 32, HEADS), jnp.int32),
        pltpu.VMEM((ROWS, WIDTH), BF),
        pltpu.VMEM((GROUPS, ROWS + 4 * RIM, LANES), F32),
        pltpu.VMEM((GROUPS, ROWS + 2 * RIM, LANES), F32),
        pltpu.VMEM((GROUPS, ROWS + 2 * RIM, LANES), F32),
        pltpu.VMEM((GROUPS, ROWS, LANES), F32),
        pltpu.VMEM((2, 2 * RIM, WIDTH), BF),
        pltpu.VMEM((2, RIM, WIDTH), BF),
        pltpu.VMEM((HEADS, ROWS), F32),
        pltpu.VMEM((TAPS, WIDTH), F32),
        pltpu.VMEM((16, WIDTH), F32),
        pltpu.VMEM((16, 1, WIDTH), F32),
        pltpu.VMEM((16, 1, WIDTH), F32),
        pltpu.VMEM((1, WIDTH), F32),
        pltpu.VMEM((4, 1, WIDTH), F32),
        pltpu.VMEM((1, WIDTH), F32),
        pltpu.VMEM((4, 1, WIDTH), F32),
        pltpu.VMEM((1, WIDTH), F32),
        pltpu.VMEM((16, 1, WIDTH), F32),
        pltpu.VMEM((16, 1, WIDTH), F32),
        *[pltpu.VMEM((WIDTH, ROWS), BF) for _ in range(4)],
        *[pltpu.VMEM((HD, SEG), BF) for _ in range(4)],
        *[pltpu.VMEM((SEG, LANES), BF) for _ in range(3)],
        *[pltpu.VMEM((LANES, SEG), BF) for _ in range(2)],
        pltpu.VMEM((SEG, SEG), BF),
        pltpu.VMEM((SEG, SEG), BF),
        pltpu.VMEM((2, QB, SEG), F32),
        pltpu.VMEM((SEG, 1), F32),
        pltpu.VMEM((HD, SEG), BF),
        pltpu.VMEM((HD, SEG), BF),
        *[pltpu.VMEM((HD, SEG), BF) for _ in range(3)],
        dma((4,)),
        dma((4,)),
        dma((3,)),
        dma((3,)),
        dma((2, 2)),
        dma((2, 2)),
        dma((6,)),
        dma((6,)),
        dma((7,)),
        dma((4,)),
    ]
    hbm = pl.BlockSpec(memory_space=pl.ANY)
    turned = jax.ShapeDtypeStruct((WIDTH, ROWS), BF)
    taps_out = jax.ShapeDtypeStruct((TAPS, WIDTH), F32)
    dq, dk, dv, gb, gk = pl.pallas_call(
        kernel,
        out_shape=(turned, turned, turned, local, taps_out),
        in_specs=[hbm] * 7 + [smem],
        out_specs=(hbm,) * 4 + (vmem,),
        scratch_shapes=scratch,
        compiler_params=pltpu.CompilerParams(
            collective_id=0, has_side_effects=True, vmem_limit_bytes=56 * 1024 * 1024
        ),
        cost_estimate=pl.CostEstimate(
            flops=5 * 2 * SEG * SEG * HD, bytes_accessed=4 << 20, transcendentals=SEG * SEG
        ),
    )(queries, key_rows, value_rows, block_in, grad_out, conv_kernel, drop_bits, seg_length)

    def finish(dq_i, dk_i, dv_i, gb_i, gk_i, dq_o, dk_o, dv_o, gb_o, gk_o):
        for src, dst in ((dq_i, dq_o), (dk_i, dk_o), (dv_i, dv_o)):
            for j in range(dst.shape[1] // LANES):
                s = slice(j * LANES, (j + 1) * LANES)
                dst[:, s] = src[s, :].T
        gb_o[...] = gb_i[...]
        gk_o[...] = gk_i[...]

    wide = 8 * HD
    by_rows = pl.BlockSpec((wide, ROWS), lambda i: (i, 0))
    by_columns = pl.BlockSpec((ROWS, wide), lambda i: (0, i))
    taps_columns = pl.BlockSpec((TAPS, wide), lambda i: (0, i))
    return pl.pallas_call(
        finish,
        grid=(WIDTH // wide,),
        out_shape=(local, local, local, local, taps_out),
        in_specs=[by_rows] * 3 + [by_columns, taps_columns],
        out_specs=[by_columns] * 4 + [taps_columns],
    )(dq, dk, dv, gb, gk)


def solution(mesh):
    split = P(("ctx", "seq"), None)
    return jax.shard_map(
        on_device,
        mesh=mesh,
        in_specs=(split, split, split, split, split, P(), split, P("ctx")),
        out_specs=(split, split, split, split, P()),
        check_vma=False,
    )
```
